256 devices in a mesh: chan: 16 (over z, x_lo), freq: 16 (over x_hi, y, core).
Axes of the slice: x: 4 (x_hi: 2, x_lo: 2; x = x_hi * 2 + x_lo), y: 4, z: 8, core: 2. Of those that a mesh axis runs over, the one named last changes fastest.
Arguments:
- traces: bfloat16 [2048, 36864], P('chan', 'freq'), may hold values from -60 to 60
- starts: int32 [16], P('freq'), may hold values from 0 to 256
- mask: int32 [2048], P('chan'), may hold values 0 or 1
- pair_offsets: int32 [16, 3], P('chan'), may hold values from 0 to 8, as said below
Outputs:
- correlations: bfloat16 [16, 3, 128, 128, 1024], P('chan', None, 'freq')
The draws below stay inside these ranges and needn't reach their ends.
Inputs may be any that keep to these rules, and one draw needn't show every extreme that they name: `pair_offsets`: each row holds 3 different offsets.
All inputs are finite; a program needn't handle non-finite values. No bound on the sum of `mask` on one device may be relied on, other than what follows from the above.
Results may differ from the reference program's by a relative error of at most 0.0066.
Values may be sent and summed in bfloat16 or wider, within the bound.
A program may use at most 128 MiB of HBM per device.

```python
import math
import jax
import jax.numpy as jnp
from jax import lax

BLK = 128
NB = 16
C = 2048
W = 16
L = 2048
SLACK = 256
SEG = 2304
F = 512
KLO = 128
LAGS = 1024
K = 3
OFF = 8


def draw_traces(key, part):
    key = jax.random.fold_in(key, 5)
    noise_key, scale_key = jax.random.split(key, 2)
    noise = jnp.clip(jax.random.normal(noise_key, (C, W, SEG), jnp.float32), -6.0, 6.0)
    spread_log = math.log(10.0)
    amplitude = jnp.exp(jax.random.uniform(scale_key, (C, W, 1), jnp.float32) * spread_log)
    return (noise * amplitude).reshape(C, W * SEG).astype(jnp.bfloat16)


def draw_starts(key, part):
    key = jax.random.fold_in(key, 7)
    values = jax.random.randint(key, (W,), 0, SLACK + 1, jnp.int32)
    return values.at[0].set(SLACK).at[1].set(0)


def draw_pair_offsets(key, part):
    key = jax.random.fold_in(key, 11)
    scores = jax.random.randint(key, (NB, OFF + 1), 0, 1000, jnp.int32) * 16 + jnp.arange(OFF + 1, dtype=jnp.int32)[None, :]
    scores = scores.at[0, OFF].add(1000000).at[1, 0].add(1000000)
    chosen = jax.lax.top_k(scores, K)[1]
    return chosen.astype(jnp.int32)


def set_ends(array, stream_key, least, largest):
    longest = array.shape.index(max(array.shape))
    spots = []
    for shift in (0, 1):
        where = [jax.random.randint(jax.random.fold_in(stream_key, axis), (), 0, length) for axis, length in enumerate(array.shape)]
        where[longest] = (where[longest] + shift) % array.shape[longest]
        spots.append(tuple(where))
    return array.at[spots[0]].set(least).at[spots[1]].set(largest)


def setup_inputs(seed: int = 0) -> dict:
    streams_of = jax.random.split(jax.random.key(seed), 5)
    traces = draw_traces(jax.random.fold_in(streams_of[4], 71), 0)
    starts = draw_starts(jax.random.fold_in(streams_of[4], 71), 0)
    mask = set_ends((jax.random.randint(streams_of[2], (C,), 0, 8) < 7).astype(jnp.int32), jax.random.fold_in(streams_of[2], 1), 0, 1)
    pair_offsets = draw_pair_offsets(jax.random.fold_in(streams_of[4], 71), 0)
    return dict(traces=traces, starts=starts, mask=mask, pair_offsets=pair_offsets)


def dft_table():
    samples = jnp.arange(L, dtype=jnp.int32)
    bin_ids = KLO + jnp.arange(F, dtype=jnp.int32)
    phase_idx = samples[:, None] * bin_ids[None, :] % L
    angles = 2.0 * math.pi / L * phase_idx.astype(jnp.float32)
    window_taper = 0.5 - 0.5 * jnp.cos(2.0 * math.pi / L * samples.astype(jnp.float32))
    real_cols = window_taper[:, None] * jnp.cos(angles)
    imag_cols = -window_taper[:, None] * jnp.sin(angles)
    return jnp.concatenate([real_cols, imag_cols], axis=1).astype(jnp.bfloat16)

def lag_table():
    bin_ids = KLO + jnp.arange(F, dtype=jnp.int32)
    delays = jnp.arange(LAGS, dtype=jnp.int32) - LAGS // 2
    phase_idx = bin_ids[:, None] * delays[None, :] % L
    angles = 2.0 * math.pi / L * phase_idx.astype(jnp.float32)
    return jnp.stack([jnp.cos(angles), -jnp.sin(angles)]).astype(jnp.bfloat16)

def cross_spectra(left_rows, right_rows):
    left_rows = left_rows.astype(jnp.float32)
    right_rows = right_rows.astype(jnp.float32)
    real_part = jnp.einsum('iwf,jwf->fij', left_rows[:, :, 0], right_rows[:, :, 0]) + jnp.einsum('iwf,jwf->fij', left_rows[:, :, 1], right_rows[:, :, 1])
    imag_part = jnp.einsum('iwf,jwf->fij', left_rows[:, :, 1], right_rows[:, :, 0]) - jnp.einsum('iwf,jwf->fij', left_rows[:, :, 0], right_rows[:, :, 1])
    return jnp.stack([real_part, imag_part])

def reference(traces, starts, mask, pair_offsets):
    windows = traces.reshape(C, W, SEG)
    segments = jax.vmap(lambda trace_rows, begin_at: lax.dynamic_slice_in_dim(trace_rows, begin_at, L, 1), in_axes=(1, 0), out_axes=1)(windows, starts)
    spectra = jnp.dot(segments.reshape(C * W, L), dft_table(), preferred_element_type=jnp.float32).reshape(C, W, 2, F)
    power_mean = lax.optimization_barrier(jnp.sum(spectra * spectra, axis=(2, 3))) / F
    weight = lax.rsqrt(power_mean + 1e-06) * mask.astype(jnp.float32)[:, None]
    whitened = (spectra * weight[:, :, None, None]).astype(jnp.bfloat16)
    padded = jnp.concatenate([whitened, jnp.zeros((OFF * BLK, W, 2, F), jnp.bfloat16)], axis=0)
    lag_basis = lag_table().astype(jnp.float32)
    lag_scale = 1.0 / (W * math.sqrt(F))

    def one_pair(item_no):
        block_no = item_no // K
        slot_no = item_no % K
        offset = pair_offsets[block_no, slot_no]
        left_rows = lax.dynamic_slice_in_dim(whitened, (block_no * BLK).astype(jnp.int32), BLK, 0)
        right_rows = lax.dynamic_slice_in_dim(padded, ((block_no + offset) * BLK).astype(jnp.int32), BLK, 0)
        rounded = lax.optimization_barrier(cross_spectra(left_rows, right_rows).astype(jnp.bfloat16))
        lagged = jnp.einsum('rfij,rfm->ijm', rounded.astype(jnp.float32), lag_basis) * lag_scale
        return lagged.astype(jnp.bfloat16)
    result = lax.map(one_pair, jnp.arange(NB * K, dtype=jnp.int32))
    return result.reshape(NB, K, BLK, BLK, LAGS)
```

```python
import functools
import math

import jax
import jax.numpy as jnp
import ml_dtypes
import numpy as np
from jax import lax
from jax.experimental import pallas as pl
from jax.experimental.pallas import tpu as pltpu
from jax.sharding import PartitionSpec as P

BLK = 128
NB = 16
W = 16
L = 2048
SEG = 2304
F = 512
KLO = 128
LAGS = 1024
K = 3
ROWS = 2 * F
NQ = 4
RQ = ROWS // NQ
GQ = RQ // 16
MESH = pl.DeviceIdType.MESH
BF16 = jnp.bfloat16
F32 = jnp.float32


def dft_table():
    samples = np.arange(L, dtype=np.int64)
    bin_ids = KLO + np.arange(F, dtype=np.int64)
    angles = 2.0 * np.pi / L * (samples[:, None] * bin_ids[None, :] % L)
    taper = 0.5 - 0.5 * np.cos(2.0 * np.pi / L * samples)
    both = np.stack([taper[:, None] * np.cos(angles), -taper[:, None] * np.sin(angles)], axis=2)
    return both.reshape(L, ROWS).astype(np.float32).astype(ml_dtypes.bfloat16)


def lag_table():
    bin_ids = KLO + np.arange(F, dtype=np.int64)
    delays = np.arange(LAGS, dtype=np.int64) - LAGS // 2
    angles = 2.0 * np.pi / L * (bin_ids[:, None] * delays[None, :] % L)
    both = np.stack([np.cos(angles), -np.sin(angles)], axis=1)
    return both.reshape(ROWS, LAGS).astype(np.float32).astype(ml_dtypes.bfloat16)


def spectra_kernel(start_ref, traces_ref, mask_ref, basis_ref, by_bin_ref, by_owner_ref):
    shifted = pltpu.roll(traces_ref[...].astype(F32), lax.rem(SEG - start_ref[0], SEG), 1)
    segment = shifted[:, :L].astype(BF16)
    spectra = jnp.dot(segment, basis_ref[...], preferred_element_type=F32)
    power_mean = jnp.sum(spectra * spectra, axis=1, keepdims=True) / F
    weight = lax.rsqrt(power_mean + 1e-06) * mask_ref[...].astype(F32)
    whitened = spectra * weight
    by_bin_ref[...] = whitened.T.astype(BF16)
    for owner in range(16):
        rows = whitened[8 * owner : 8 * owner + 8]
        by_owner_ref[owner] = jnp.concatenate([rows[:, :F], rows[:, F:]], axis=0).astype(BF16)


def pairs_kernel(
    offsets_ref, own_ref, by_owner_ref, out_ref,
    near0, near1, near2, near3, held, rows_in, left, terms, turned,
    chain_send, chain_recv, side_send, side_recv, own_send, own_recv, pass_send, pass_recv, out_sem,
):
    near = [near0, near1, near2, near3]
    chan = lax.axis_index("chan")
    freq = lax.axis_index("freq")
    x_lo = lax.rem(chan, 2)
    core = lax.rem(freq, 2)
    y = lax.rem(freq // 2, 4)
    x_hi = freq // 8

    def window(hi, at_y, at_core):
        return hi * 8 + lax.rem(at_y, 4) * 2 + at_core

    below = (lax.rem(chan + 14, 16), freq)
    above = (lax.rem(chan + 2, 16), freq)
    beside = (chan + 1 - 2 * x_lo, freq)
    sibling = (chan, window(x_hi, y, 1 - core))
    across = (chan, window(1 - x_hi, y, core))
    y_up = (chan, window(x_hi, y + 1, core))
    y_down = (chan, window(x_hi, y + 3, core))
    peers = [(chan, lax.rem(freq + shift, 16)) for shift in range(1, 16)]

    barrier = pltpu.get_barrier_semaphore()
    everyone = peers + [below, above, beside]
    for other in everyone:
        pl.semaphore_signal(barrier, inc=1, device_id=other, device_id_type=MESH)
    for q in range(NQ):
        near[q][0] = own_ref[RQ * q : RQ * (q + 1), :]
    rows_in[freq] = by_owner_ref[freq]
    pl.semaphore_wait(barrier, len(everyone))

    def remote(src, dst, send, recv, device):
        return pltpu.make_async_remote_copy(
            src_ref=src, dst_ref=dst, send_sem=send, recv_sem=recv, device_id=device, device_id_type=MESH
        )

    def chain(hop, q):
        return remote(near[q].at[hop - 1], near[q].at[hop], chain_send.at[q, hop - 1], chain_recv.at[q, hop - 1], below)

    def side(hop, q):
        return remote(near[q].at[hop - x_lo], near[q].at[4 + hop], side_send.at[q, hop - 1], side_recv.at[q, hop - 1], beside)

    def owner_rows(shift):
        there = lax.rem(freq + shift, 16)
        return remote(by_owner_ref.at[there], rows_in.at[freq], own_send.at[shift - 1], own_recv.at[shift - 1], (chan, there))

    def wave(step):
        for q in range(NQ):
            hop = step - 2 * q
            if hop == 0:
                chain(1, q).start()
            if 1 <= hop <= 4:
                chain(hop, q).wait_recv()
                if hop < 4:
                    chain(hop + 1, q).start()
                side(hop, q).start()

    mine = window(x_hi, y, core)
    other_hi = window(1 - x_hi, y, core)

    own_before = window(x_hi, y + 3, core)
    own_after = window(x_hi, y + 1, core)
    other_before = window(1 - x_hi, y + 3, core)
    other_after = window(1 - x_hi, y + 1, core)
    own_far = window(x_hi, y + 2, core)
    other_far = window(1 - x_hi, y + 2, core)
    table = [
        (mine, across), (mine, y_up), (mine, y_down), (other_hi, y_up), (other_hi, y_down),
        (own_before, y_up), (other_after, y_down),
        (mine, sibling), (other_hi, sibling), (own_before, sibling), (own_after, sibling),
        (other_before, sibling), (other_after, sibling), (own_far, sibling), (other_far, sibling),
    ]

    def spread(q, no):
        which, device = table[no]
        return remote(held.at[q, which], held.at[q, which], pass_send.at[q, no], pass_recv.at[q, no], device)

    def phase_a(q):
        for hop in range(1, 5):
            side(hop, q).wait_recv()
        for slot in range(K):
            offset = offsets_ref[slot]
            odd = lax.rem(offset, 2)
            place = offset // 2 + odd * 5
            rows = near[q][place]
            held[q, mine, slot] = jnp.where(chan + offset < NB, rows, jnp.zeros_like(rows))
        for no in (0, 1, 2, 7):
            spread(q, no).start()

    def phase_b(q):
        spread(q, 0).wait_recv()
        for no in (3, 4, 8):
            spread(q, no).start()

    def phase_c(q):
        spread(q, 1).wait_recv()
        spread(q, 5).start()
        spread(q, 9).start()
        spread(q, 2).wait_recv()
        spread(q, 10).start()
        spread(q, 4).wait_recv()
        spread(q, 6).start()
        spread(q, 12).start()
        spread(q, 3).wait_recv()
        spread(q, 11).start()

    def phase_d(q):
        spread(q, 5).wait_recv()
        spread(q, 13).start()
        spread(q, 6).wait_recv()
        spread(q, 14).start()

    def out_copy(q):
        return pltpu.make_async_copy(turned.at[q % 2], out_ref.at[:, :, pl.ds(RQ * q, RQ)], out_sem.at[q % 2])

    def phase_e(q):
        for no in range(7, 15):
            spread(q, no).wait_recv()

        def group(g, carry):
            at = pl.ds(pl.multiple_of(g * 16, 16), 16)
            right = jnp.concatenate([held[q, :, slot, at, :].reshape(256, BLK) for slot in range(K)], axis=1)
            both = jnp.dot(left[q * GQ + g], right, preferred_element_type=F32)
            for slot in range(K):
                terms[slot, :, at, :] = both[:, BLK * slot : BLK * (slot + 1)].astype(BF16).reshape(8, 16, BLK)
            return carry

        lax.fori_loop(0, GQ, group, 0)
        if q >= 2:
            out_copy(q - 2).wait()

        def turn(n, carry):
            turned[q % 2, n] = terms[n // 8, lax.rem(n, 8)].T
            return carry

        lax.fori_loop(0, K * 8, turn, 0)
        out_copy(q).start()

    def build_left():
        for shift in range(1, 16):
            owner_rows(shift).wait_recv()
        lane = lax.broadcasted_iota(jnp.int32, (16, 128), 1)
        row = lax.broadcasted_iota(jnp.int32, (16, 128), 0)
        same_bin = (lane % 16) // 2 == row // 2
        even_row = row % 2 == 0
        slab = lane // 16
        even_lane = lane % 2 == 0

        def step(n, carry):
            v = n // 8
            s = lax.rem(n, 8)
            for half in range(2):
                got = jnp.zeros((16, 128), F32)
                for w in range(8):
                    part = rows_in[half * 8 + w, :, pl.ds(pl.multiple_of(v * 128, 128), 128)].astype(F32)
                    got = jnp.where(slab == w, pltpu.roll(part, lax.rem(16 * (w + 8 - s), 128), 1), got)
                swapped = jnp.where(even_lane, pltpu.roll(got, 127, 1), -pltpu.roll(got, 1, 1))
                for h in range(2):
                    for i in range(8):
                        r = slice(h * 8 + i, h * 8 + i + 1)
                        value = jnp.where(even_row, got[r], swapped[r])
                        left[h * 32 + n, 16 * i : 16 * i + 16, 128 * half : 128 * half + 128] = jnp.where(
                            same_bin, value, 0.0
                        ).astype(BF16)
            return carry

        lax.fori_loop(0, 32, step, 0)

    wave(0)
    for shift in range(1, 16):
        owner_rows(shift).start()
    wave(1)
    wave(2)
    wave(3)
    wave(4)
    phase_a(0)
    phase_b(0)
    wave(5)
    build_left()
    wave(6)
    phase_a(1)
    phase_c(0)
    phase_b(1)
    wave(7)
    phase_d(0)
    wave(8)
    phase_a(2)
    phase_c(1)
    phase_e(0)
    phase_b(2)
    wave(9)
    phase_d(1)
    wave(10)
    phase_a(3)
    phase_c(2)
    phase_e(1)
    phase_b(3)
    phase_d(2)
    phase_c(3)
    phase_e(2)
    phase_d(3)
    phase_e(3)

    for q in range(NQ):
        for hop in range(1, 5):
            chain(hop, q).wait_send()
            side(hop, q).wait_send()
        for no in range(len(table)):
            spread(q, no).wait_send()
    for shift in range(1, 16):
        owner_rows(shift).wait_send()
    out_copy(2).wait()
    out_copy(3).wait()


def on_device(traces, starts, mask, pair_offsets):
    vmem = pl.BlockSpec(memory_space=pltpu.VMEM)
    smem = pl.BlockSpec(memory_space=pltpu.SMEM)
    by_bin, by_owner = pl.pallas_call(
        spectra_kernel,
        name="spectra",
        out_shape=(jax.ShapeDtypeStruct((ROWS, BLK), BF16), jax.ShapeDtypeStruct((16, 16, F), BF16)),
        in_specs=[smem, vmem, vmem, vmem],
        out_specs=(vmem, vmem),
        compiler_params=pltpu.CompilerParams(vmem_limit_bytes=32 * 2**20),
    )(starts, traces, mask.reshape(BLK, 1), jnp.asarray(dft_table()))
    dma = pltpu.SemaphoreType.DMA
    pair_spectra = pl.pallas_call(
        pairs_kernel,
        name="pairs",
        out_shape=jax.ShapeDtypeStruct((K * 8, BLK, ROWS), BF16),
        in_specs=[smem, vmem, vmem],
        out_specs=pl.BlockSpec(memory_space=pl.ANY),
        scratch_shapes=[pltpu.VMEM((9, RQ, BLK), BF16)] * NQ
        + [
            pltpu.VMEM((NQ, 16, K, RQ, BLK), BF16),
            pltpu.VMEM((16, 16, F), BF16),
            pltpu.VMEM((ROWS // 16, 128, 256), BF16),
            pltpu.VMEM((K, 8, RQ, BLK), BF16),
            pltpu.VMEM((2, K * 8, BLK, RQ), BF16),
            dma((NQ, 4)), dma((NQ, 4)), dma((NQ, 4)), dma((NQ, 4)),
            dma((15,)), dma((15,)), dma((NQ, 15)), dma((NQ, 15)), dma((2,)),
        ],
        compiler_params=pltpu.CompilerParams(
            collective_id=0, has_side_effects=True, vmem_limit_bytes=48 * 2**20
        ),
    )(pair_offsets.reshape(K), by_bin, by_owner)
    lagged = jnp.dot(
        pair_spectra.reshape(K * 8 * BLK, ROWS), jnp.asarray(lag_table()), preferred_element_type=F32
    )
    lag_scale = 1.0 / (W * math.sqrt(F))
    return (lagged * lag_scale).astype(BF16).reshape(1, K, 8, BLK, LAGS)


def solution(mesh):
    in_specs = (P("chan", "freq"), P("freq"), P("chan"), P("chan", None))
    out_specs = P("chan", None, "freq", None, None)
    return jax.shard_map(
        on_device, mesh=mesh, in_specs=in_specs, out_specs=out_specs, check_vma=False
    )
```

```python
import functools
import math

import jax
import jax.numpy as jnp
import ml_dtypes
import numpy as np
from jax import lax
from jax.experimental import pallas as pl
from jax.experimental.pallas import tpu as pltpu
from jax.sharding import PartitionSpec as P

BLK = 128
NB = 16
W = 16
L = 2048
SEG = 2304
F = 512
KLO = 128
LAGS = 1024
K = 3
ROWS = 2 * F
SIZES = (128, 128, 192, 192, 192, 192)
NQ = len(SIZES)
FIRST = tuple(sum(SIZES[:q]) for q in range(NQ))
TURNED = (0, 1, 2, 3)
VMEM_MIB = 60
MESH = pl.DeviceIdType.MESH
BF16 = jnp.bfloat16
F32 = jnp.float32


def dft_table():
    samples = np.arange(L, dtype=np.int64)
    bin_ids = KLO + np.arange(F, dtype=np.int64)
    angles = 2.0 * np.pi / L * (samples[:, None] * bin_ids[None, :] % L)
    taper = 0.5 - 0.5 * np.cos(2.0 * np.pi / L * samples)
    both = np.stack([taper[:, None] * np.cos(angles), -taper[:, None] * np.sin(angles)], axis=2)
    return both.reshape(L, ROWS).astype(np.float32).astype(ml_dtypes.bfloat16)


def lag_table():
    bin_ids = KLO + np.arange(F, dtype=np.int64)
    delays = np.arange(LAGS, dtype=np.int64) - LAGS // 2
    angles = 2.0 * np.pi / L * (bin_ids[:, None] * delays[None, :] % L)
    both = np.stack([np.cos(angles), -np.sin(angles)], axis=1)
    return both.reshape(ROWS, LAGS).astype(np.float32).astype(ml_dtypes.bfloat16)


class Tracked:
    def __init__(self, key, copy, started, waited):
        self.key, self.copy, self.started, self.waited = key, copy, started, waited

    def start(self):
        self.copy.start()
        self.started[self.key] = self.copy

    def wait_recv(self):
        self.copy.wait_recv()
        self.waited.add(self.key)


SCHEDULE = (
    "s0", "o", "w10", "s1", "w20", "l0", "w11", "s2", "l1", "w30", "l2", "w21", "l3", "w12", "s3", "w40", "w31",
    "w22", "w13", "s4", "a0", "w41", "w32", "w23", "w14", "s5", "a1", "b0", "c0", "C0", "w42", "w33", "w24",
    "w15", "b1", "c1", "C1", "w43", "a2", "w34", "k0", "K0", "w25", "d0", "a3", "w44", "k1", "K1", "w35", "d1",
    "b2", "w45", "h0", "c2", "C2", "a4", "e0", "f00", "b3", "c3", "C3", "f01", "h1", "a5", "k2", "K2", "e1",
    "f10", "b4", "d2", "f11", "c4", "C4", "b5", "k3", "K3", "h2", "d3", "e2", "f20", "c5", "C5", "f21", "h3",
    "k4", "K4", "e3", "f30", "d4", "k5", "f31", "h4", "K5", "e4", "f40", "d5", "h5", "f41", "e5", "f50", "f51",
)


def correlate_kernel(
    schedule, starts_hbm, traces_hbm, mask_hbm, offsets_hbm, basis_hbm, lag_hbm, out_ref,
    *scratch,
):
    near = scratch[:NQ]
    held = scratch[NQ : 2 * NQ]
    theirs = scratch[2 * NQ : 3 * NQ]
    (
        by_owner, rows_in, left, terms, total, done, out_sem,
        starts_ref, traces_ref, mask_ref, offsets_ref, beside_offsets, lag_ref, load_sem, asked_send, asked_recv,
        chain_send, chain_recv, side_send, side_recv, own_send, own_recv, pass_send, pass_recv,
    ) = scratch[3 * NQ :]
    basis_ref = left
    operands = [
        (starts_hbm, starts_ref), (traces_hbm, traces_ref), (mask_hbm, mask_ref),
        (basis_hbm, basis_ref), (offsets_hbm, offsets_ref), (lag_hbm, lag_ref),
    ]
    loads = [pltpu.make_async_copy(src, dst, load_sem.at[no]) for no, (src, dst) in enumerate(operands)]
    for load in loads:
        load.start()
    chan = lax.axis_index("chan")
    freq = lax.axis_index("freq")
    x_lo = lax.rem(chan, 2)
    core = lax.rem(freq, 2)
    y = lax.rem(freq // 2, 4)
    x_hi = freq // 8

    def window(hi, at_y, at_core):
        return hi * 8 + lax.rem(at_y, 4) * 2 + at_core

    below = (lax.rem(chan + 14, 16), freq)
    above = (lax.rem(chan + 2, 16), freq)
    beside = (chan + 1 - 2 * x_lo, freq)
    sibling = (chan, window(x_hi, y, 1 - core))
    across = (chan, window(1 - x_hi, y, core))
    diagonal = (chan + 1 - 2 * x_lo, window(1 - x_hi, y, core))
    y_up = (chan, window(x_hi, y + 1, core))
    y_down = (chan, window(x_hi, y + 3, core))
    peers = [(chan, lax.rem(freq + shift, 16)) for shift in range(1, 16)]

    started, waited = {}, set()
    barrier = pltpu.get_barrier_semaphore()
    everyone = peers + [below, above, beside, diagonal]
    for other in everyone:
        pl.semaphore_signal(barrier, inc=1, device_id=other, device_id_type=MESH)
    for load in loads[:4]:
        load.wait()
    shifted = pltpu.roll(traces_ref[...].astype(F32), lax.rem(SEG - starts_ref[0], SEG), 1)
    spectra = jnp.dot(shifted[:, :L].astype(BF16), basis_ref[...], preferred_element_type=F32)
    power_mean = jnp.sum(spectra * spectra, axis=1, keepdims=True) / F
    working = jnp.broadcast_to(mask_ref[...].astype(F32), (BLK, BLK)).T[:, :1]
    whitened = spectra * (lax.rsqrt(power_mean + 1e-06) * working)
    by_bin = whitened.T.astype(BF16)
    for q in range(NQ):
        near[q][0] = by_bin[FIRST[q] : FIRST[q] + SIZES[q], :]
    for owner in range(16):
        rows = whitened[8 * owner : 8 * owner + 8]
        by_owner[owner] = jnp.concatenate([rows[:, :F], rows[:, F:]], axis=0).astype(BF16)
    rows_in[freq] = by_owner[freq]
    loads[4].wait()
    loads[5].wait()
    pl.semaphore_wait(barrier, len(everyone))

    def remote(key, src, dst, send, recv, device):
        copy = pltpu.make_async_remote_copy(
            src_ref=src, dst_ref=dst, send_sem=send, recv_sem=recv, device_id=device, device_id_type=MESH
        )
        return Tracked(key, copy, started, waited)

    def chain(hop, q):
        return remote(("chain", hop, q), near[q].at[hop - 1], near[q].at[hop], chain_send.at[q, hop - 1], chain_recv.at[q, hop - 1], below)

    def side(hop, q):
        return remote(("side", hop, q), near[q].at[hop], near[q].at[5 + hop], side_send.at[q, hop], side_recv.at[q, hop], beside)

    def owner_rows(shift):
        there = lax.rem(freq + shift, 16)
        return remote(("own", shift), by_owner.at[there], rows_in.at[freq], own_send.at[shift - 1], own_recv.at[shift - 1], (chan, there))

    def begin(q):
        chain(1, q).start()
        side(0, q).start()

    def pass_on(hop, q):
        chain(hop, q).wait_recv()
        if hop < 4:
            chain(hop + 1, q).start()
        side(hop, q).start()

    mine = window(x_hi, y, core)
    other_hi = window(1 - x_hi, y, core)

    own_before = window(x_hi, y + 3, core)
    own_after = window(x_hi, y + 1, core)
    other_before = window(1 - x_hi, y + 3, core)
    other_after = window(1 - x_hi, y + 1, core)
    own_far = window(x_hi, y + 2, core)
    other_far = window(1 - x_hi, y + 2, core)
    table = [
        (mine, diagonal), (mine, y_up), (mine, y_down), (other_hi, y_up), (other_hi, y_down),
        (own_before, y_up), (other_after, y_down),
        (mine, sibling), (other_hi, sibling), (own_before, sibling), (own_after, sibling),
        (other_before, sibling), (other_after, sibling), (own_far, sibling), (other_far, sibling),
        (own_before, y_up), (own_after, y_down), (own_far, across),
    ]

    def spread(q, no):
        which, device = table[no]
        src = dst = held[q].at[which]
        half = SIZES[q] // 2
        if no == 0:
            src = theirs[q]
        elif no == 15:
            src = dst = held[q].at[which, :, pl.ds(0, half)]
        elif no == 16:
            src = dst = held[q].at[which, :, pl.ds(half, half)]
        return remote(("spread", q, no), src, dst, pass_send.at[q, no], pass_recv.at[q, no], device)

    def ask():
        return remote(("ask",), offsets_ref, beside_offsets, asked_send.at[0], asked_recv.at[0], beside)

    def choose(q):
        for hop in range(5):
            side(hop, q).wait_recv()
        if q == 0:
            ask().wait_recv()
        for slot in range(K):
            offset = beside_offsets[0, slot]
            odd = lax.rem(offset, 2)
            place = offset // 2 + 5 - odd * (4 + x_lo)
            rows = near[q][place]
            theirs[q][slot] = jnp.where(chan + 1 - 2 * x_lo + offset < NB, rows, jnp.zeros_like(rows))
        spread(q, 0).start()
        for slot in range(K):
            offset = offsets_ref[0, slot]
            odd = lax.rem(offset, 2)
            place = offset // 2 + odd * (5 + x_lo)
            rows = near[q][place]
            held[q][mine, slot] = jnp.where(chan + offset < NB, rows, jnp.zeros_like(rows))
        for no in (1, 2, 7):
            spread(q, no).start()

    def other_in(q):
        spread(q, 0).wait_recv()
        for no in (3, 4, 8):
            spread(q, no).start()

    def own_before_in(q):
        spread(q, 1).wait_recv()
        spread(q, 15 if q in TURNED else 5).start()
        spread(q, 9).start()

    def own_after_in(q):
        spread(q, 2).wait_recv()
        if q in TURNED:
            spread(q, 16).start()
        spread(q, 10).start()

    def other_after_in(q):
        spread(q, 4).wait_recv()
        if q not in TURNED:
            spread(q, 6).start()
        spread(q, 12).start()

    def other_before_in(q):
        spread(q, 3).wait_recv()
        spread(q, 11).start()

    def own_far_in(q):
        if q in TURNED:
            spread(q, 15).wait_recv()
            spread(q, 16).wait_recv()
            spread(q, 17).start()
        else:
            spread(q, 5).wait_recv()
        spread(q, 13).start()

    def other_far_in(q):
        spread(q, 17 if q in TURNED else 6).wait_recv()
        spread(q, 14).start()

    def pair_terms(q):
        for no in range(7, 15):
            spread(q, no).wait_recv()

        def group(g, carry):
            at = pl.ds(pl.multiple_of(g * 16, 16), 16)
            right = jnp.concatenate([held[q][:, slot, at, :].reshape(256, BLK) for slot in range(K)], axis=1)
            no = FIRST[q] // 16 + g
            tile = left[
                pl.ds(pl.multiple_of(no // 4 * 128, 128), 128), pl.ds(pl.multiple_of(lax.rem(no, 4) * 256, 256), 256)
            ]
            both = jnp.dot(tile, right, preferred_element_type=F32)
            for slot in range(K):
                terms[q % 2, slot, :, at, :] = both[:, BLK * slot : BLK * (slot + 1)].astype(BF16).reshape(8, 16, BLK)
            return carry

        lax.fori_loop(0, SIZES[q] // 16, group, 0, unroll=4)

    lag_scale = 1.0 / (W * math.sqrt(F))

    def out_copy(m):
        at = pl.ds(m * 4, 4)
        return pltpu.make_async_copy(done.at[at], out_ref.at[at], out_sem.at[m])

    def lag_sums(q, half):
        def lags(m, carry):
            at = pl.ds(m * 4, 4)
            part = jnp.concatenate([terms[q % 2, m // 2, lax.rem(m, 2) * 4 + n, : SIZES[q], :].T for n in range(4)], axis=0)
            part = jnp.dot(part, lag_ref[FIRST[q] : FIRST[q] + SIZES[q], :], preferred_element_type=F32)
            part = part.reshape(4, BLK, LAGS)
            if q > 0:
                part = total[at] + part
            if q < NQ - 1:
                total[at] = part
            else:
                done[at] = (part * lag_scale).astype(BF16)
                out_copy(m).start()
            return carry

        lax.fori_loop(K * half, K * half + K, lags, 0)
        if q == NQ - 1 and half == 1:
            for m in range(K * 2):
                out_copy(m).wait()

    def build_left(v):
        if v == 0:
            for shift in range(1, 16):
                owner_rows(shift).wait_recv()
        lane = lax.broadcasted_iota(jnp.int32, (16, 128), 1)
        row = lax.broadcasted_iota(jnp.int32, (16, 128), 0)
        same_bin = (lane % 16) // 2 == row // 2
        even_row = row % 2 == 0
        slab = lane // 16
        even_lane = lane % 2 == 0

        def step(s, carry):
            for half in range(2):
                got = jnp.zeros((16, 128), F32)
                for w in range(8):
                    part = rows_in[half * 8 + w, :, 128 * v : 128 * v + 128].astype(F32)
                    got = jnp.where(slab == w, pltpu.roll(part, lax.rem(16 * (w + 8 - s), 128), 1), got)
                swapped = jnp.where(even_lane, pltpu.roll(got, 127, 1), -pltpu.roll(got, 1, 1))
                for h in range(2):
                    for i in range(8):
                        r = slice(h * 8 + i, h * 8 + i + 1)
                        value = jnp.where(even_row, got[r], swapped[r])
                        no = h * 32 + v * 8 + s
                        left[
                            pl.ds(pl.multiple_of(no // 4 * 128 + 16 * i, 16), 16),
                            pl.ds(pl.multiple_of(lax.rem(no, 4) * 256 + 128 * half, 128), 128),
                        ] = jnp.where(same_bin, value, 0.0).astype(BF16)
            return carry

        lax.fori_loop(0, 8, step, 0, unroll=2)

    def own_start():
        ask().start()
        for shift in range(1, 16):
            owner_rows(shift).start()

    steps = dict(
        s=begin, w=pass_on, o=own_start, a=choose, b=other_in, c=own_before_in, C=own_after_in, k=other_after_in,
        K=other_before_in, d=own_far_in, h=other_far_in, l=build_left, e=pair_terms, f=lag_sums,
    )
    for item in schedule:
        steps[item[0]](*[int(digit) for digit in item[1:]])
    for key, copy in started.items():
        if key not in waited:
            copy.wait_recv()
        copy.wait_send()

def correlations_of(traces, starts, mask, pair_offsets, basis, lag_basis, schedule=SCHEDULE, name="correlate", collective_id=0):
    dma = pltpu.SemaphoreType.DMA
    return pl.pallas_call(
        functools.partial(correlate_kernel, schedule),
        name=name,
        out_shape=jax.ShapeDtypeStruct((K * 8, BLK, LAGS), BF16),
        in_specs=[pl.BlockSpec(memory_space=pl.ANY)] * 6,
        out_specs=pl.BlockSpec(memory_space=pl.ANY),
        scratch_shapes=[pltpu.VMEM((10, size, BLK), BF16) for size in SIZES]
        + [pltpu.VMEM((16, K, size, BLK), BF16) for size in SIZES]
        + [pltpu.VMEM((K, size, BLK), BF16) for size in SIZES]
        + [
            pltpu.VMEM((16, 16, F), BF16),
            pltpu.VMEM((16, 16, F), BF16),
            pltpu.VMEM((L, ROWS), BF16),
            pltpu.VMEM((2, K, 8, max(SIZES), BLK), BF16),
            pltpu.VMEM((K * 8, BLK, LAGS), F32),
            pltpu.VMEM((K * 8, BLK, LAGS), BF16),
            dma((K * 2,)),
            pltpu.SMEM((1,), jnp.int32),
            pltpu.VMEM((BLK, SEG), BF16),
            pltpu.VMEM((1, BLK), jnp.int32),
            pltpu.SMEM((1, K), jnp.int32),
            pltpu.SMEM((1, K), jnp.int32),
            pltpu.VMEM((ROWS, LAGS), BF16),
            dma((6,)), dma((1,)), dma((1,)),
            dma((NQ, 4)), dma((NQ, 4)), dma((NQ, 5)), dma((NQ, 5)),
            dma((15,)), dma((15,)), dma((NQ, 18)), dma((NQ, 18)),
        ],
        compiler_params=pltpu.CompilerParams(
            collective_id=collective_id, has_side_effects=True, vmem_limit_bytes=VMEM_MIB * 2**20
        ),
    )(starts, traces, mask.reshape(1, BLK), pair_offsets, basis, lag_basis)


def deliver_kernel(src_ref, dst_ref, held, in_sem, out_sem):
    count = in_sem.shape[0]
    size = src_ref.shape[0] // count
    parts = [pl.ds(size * n, size) for n in range(count)]
    ins = [pltpu.make_async_copy(src_ref.at[p], held.at[p], in_sem.at[n]) for n, p in enumerate(parts)]
    outs = [pltpu.make_async_copy(held.at[p], dst_ref.at[p], out_sem.at[n]) for n, p in enumerate(parts)]
    for copy in ins:
        copy.start()
    for copy_in, copy_out in zip(ins, outs):
        copy_in.wait()
        copy_out.start()
    for copy in outs:
        copy.wait()


def on_device(traces, starts, mask, pair_offsets):
    out = correlations_of(traces, starts, mask, pair_offsets, jnp.asarray(dft_table()), jnp.asarray(lag_table()))
    out = pl.pallas_call(
        deliver_kernel,
        name="deliver",
        out_shape=jax.ShapeDtypeStruct(out.shape, BF16),
        in_specs=[pl.BlockSpec(memory_space=pl.ANY)],
        out_specs=pl.BlockSpec(memory_space=pl.ANY),
        scratch_shapes=[pltpu.VMEM(out.shape, BF16), pltpu.SemaphoreType.DMA((4,)), pltpu.SemaphoreType.DMA((4,))],
        compiler_params=pltpu.CompilerParams(vmem_limit_bytes=VMEM_MIB * 2**20),
    )(out)
    return out.reshape(1, K, 8, BLK, LAGS)


def solution(mesh):
    in_specs = (P("chan", "freq"), P("freq"), P("chan"), P("chan", None))
    out_specs = P("chan", None, "freq", None, None)
    return jax.shard_map(
        on_device, mesh=mesh, in_specs=in_specs, out_specs=out_specs, check_vma=False
    )
```

```python
import functools
import math

import jax
import jax.numpy as jnp
import ml_dtypes
import numpy as np
from jax import lax
from jax.experimental import pallas as pl
from jax.experimental.pallas import tpu as pltpu
from jax.sharding import PartitionSpec as P

BLK = 128
NB = 16
W = 16
L = 2048
SEG = 2304
F = 512
KLO = 128
LAGS = 1024
K = 3
ROWS = 2 * F
SIZES = (128, 128, 64, 192, 256, 128, 128)
NQ = len(SIZES)
FIRST = tuple(sum(SIZES[:q]) for q in range(NQ))
TURNED = (0, 1, 2, 3, 4)
VMEM_MIB = 60
MESH = pl.DeviceIdType.MESH
BF16 = jnp.bfloat16
F32 = jnp.float32


def dft_table():
    samples = np.arange(L, dtype=np.int64)
    bin_ids = KLO + np.arange(F, dtype=np.int64)
    angles = 2.0 * np.pi / L * (samples[:, None] * bin_ids[None, :] % L)
    taper = 0.5 - 0.5 * np.cos(2.0 * np.pi / L * samples)
    both = np.stack([taper[:, None] * np.cos(angles), -taper[:, None] * np.sin(angles)], axis=2)
    return both.reshape(L, ROWS).astype(np.float32).astype(ml_dtypes.bfloat16)


def lag_table():
    bin_ids = KLO + np.arange(F, dtype=np.int64)
    delays = np.arange(LAGS, dtype=np.int64) - LAGS // 2
    angles = 2.0 * np.pi / L * (bin_ids[:, None] * delays[None, :] % L)
    both = np.stack([np.cos(angles), -np.sin(angles)], axis=1)
    return both.reshape(ROWS, LAGS).astype(np.float32).astype(ml_dtypes.bfloat16)


class Tracked:
    def __init__(self, key, copy, started, waited):
        self.key, self.copy, self.started, self.waited = key, copy, started, waited

    def start(self):
        self.copy.start()
        self.started[self.key] = self.copy

    def wait_recv(self):
        self.copy.wait_recv()
        self.waited.add(self.key)


GROUPS = ((0, 3), (3, 5), (5, 7))
GROUP_ROWS = tuple(sum(SIZES[first:end]) for first, end in GROUPS)
LATE = GROUP_ROWS[-1]

SCHEDULE = (
    "s0", "s1", "o", "w10", "s2", "w11", "s3", "w20", "l0", "w12", "w21", "s4", "l1", "w13", "w30", "s5", "l2",
    "w22", "w31", "l3", "w14", "s6", "w23", "w40", "a0", "w15", "w32", "w41", "a1", "w24", "w16", "b0", "c0",
    "C0", "w33", "w25", "w42", "a2", "b1", "c1", "C1", "w34", "w26", "k0", "K0", "w43", "d0", "b2", "a3", "w35",
    "c2", "C2", "w44", "k1", "K1", "d1", "a4", "w36", "w45", "k2", "K2", "h0", "e0", "c3", "C3", "a5", "w46",
    "d2", "b3", "h1", "c4", "C4", "e1", "a6", "d3", "b4", "c5", "C5", "b5", "h2", "k3", "K3", "e2", "b6", "f00",
    "d4", "f01", "c6", "C6", "h3", "e3", "k4", "K4", "h4", "k5", "d5", "e4", "K5", "k6", "f10", "K6", "h5", "f11",
    "d6", "e5", "h6", "e6",
)


def correlate_kernel(
    schedule, starts_hbm, traces_hbm, mask_hbm, offsets_hbm, basis_hbm, lag_hbm, sums_ref, late_ref,
    *scratch,
):
    near = scratch[:NQ]
    held = scratch[NQ : 2 * NQ]
    theirs = scratch[2 * NQ : 3 * NQ]
    terms = scratch[3 * NQ : 3 * NQ + len(GROUPS)]
    (
        by_owner, rows_in, left, total, done, out_sem, late_sem,
        starts_ref, traces_ref, mask_ref, offsets_ref, beside_offsets, lag_ref, load_sem, asked_send, asked_recv,
        chain_send, chain_recv, side_send, side_recv, own_send, own_recv, pass_send, pass_recv,
    ) = scratch[3 * NQ + len(GROUPS) :]
    basis_ref = left
    parts = [slice(n * 512, n * 512 + 512) for n in range(4)]
    operands = [
        (starts_hbm, starts_ref), (traces_hbm, traces_ref), *[(basis_hbm.at[p], basis_ref.at[p]) for p in parts],
        (mask_hbm, mask_ref), (offsets_hbm, offsets_ref), (lag_hbm, lag_ref),
    ]
    loads = [pltpu.make_async_copy(src, dst, load_sem.at[no]) for no, (src, dst) in enumerate(operands)]
    for load in loads:
        load.start()
    chan = lax.axis_index("chan")
    freq = lax.axis_index("freq")
    x_lo = lax.rem(chan, 2)
    core = lax.rem(freq, 2)
    y = lax.rem(freq // 2, 4)
    x_hi = freq // 8

    def window(hi, at_y, at_core):
        return hi * 8 + lax.rem(at_y, 4) * 2 + at_core

    below = (lax.rem(chan + 14, 16), freq)
    above = (lax.rem(chan + 2, 16), freq)
    beside = (chan + 1 - 2 * x_lo, freq)
    sibling = (chan, window(x_hi, y, 1 - core))
    across = (chan, window(1 - x_hi, y, core))
    below_beside = (lax.rem(chan + 14, 16) + 1 - 2 * x_lo, freq)
    above_beside = (lax.rem(chan + 2, 16) + 1 - 2 * x_lo, freq)
    diagonal = (chan + 1 - 2 * x_lo, window(1 - x_hi, y, core))
    y_up = (chan, window(x_hi, y + 1, core))
    y_down = (chan, window(x_hi, y + 3, core))
    peers = [(chan, lax.rem(freq + shift, 16)) for shift in range(1, 16)]

    started, waited = {}, set()
    barrier = pltpu.get_barrier_semaphore()
    everyone = peers + [below, above, beside, diagonal, below_beside, above_beside]
    for other in everyone:
        pl.semaphore_signal(barrier, inc=1, device_id=other, device_id_type=MESH)
    loads[0].wait()
    loads[1].wait()
    shifted = pltpu.roll(traces_ref[...].astype(F32), lax.rem(SEG - starts_ref[0], SEG), 1)
    segment = shifted[:, :L].astype(BF16)
    spectra = jnp.zeros((BLK, ROWS), F32)
    for n, p in enumerate(parts):
        loads[2 + n].wait()
        spectra = spectra + jnp.dot(segment[:, p], basis_ref[p, :], preferred_element_type=F32)
    for load in loads[6:]:
        load.wait()
    power_mean = jnp.sum(spectra * spectra, axis=1, keepdims=True) / F
    working = jnp.broadcast_to(mask_ref[...].astype(F32), (BLK, BLK)).T[:, :1]
    whitened = spectra * (lax.rsqrt(power_mean + 1e-06) * working)
    by_bin = whitened.T.astype(BF16)
    for q in range(NQ):
        near[q][0] = by_bin[FIRST[q] : FIRST[q] + SIZES[q], :]
    for owner in range(16):
        rows = whitened[8 * owner : 8 * owner + 8]
        by_owner[owner] = jnp.concatenate([rows[:, :F], rows[:, F:]], axis=0).astype(BF16)
    rows_in[freq] = by_owner[freq]
    pl.semaphore_wait(barrier, len(everyone))

    def remote(key, src, dst, send, recv, device):
        copy = pltpu.make_async_remote_copy(
            src_ref=src, dst_ref=dst, send_sem=send, recv_sem=recv, device_id=device, device_id_type=MESH
        )
        return Tracked(key, copy, started, waited)

    def chain(hop, q):
        return remote(("chain", hop, q), near[q].at[hop - 1], near[q].at[hop], chain_send.at[q, hop - 1], chain_recv.at[q, hop - 1], below)

    def side(hop, q):
        src, device = (hop, beside) if hop < 4 else (3, below_beside)
        return remote(("side", hop, q), near[q].at[src], near[q].at[5 + hop], side_send.at[q, hop], side_recv.at[q, hop], device)

    def owner_rows(shift):
        there = lax.rem(freq + shift, 16)
        return remote(("own", shift), by_owner.at[there], rows_in.at[freq], own_send.at[shift - 1], own_recv.at[shift - 1], (chan, there))

    def begin(q):
        chain(1, q).start()
        side(0, q).start()

    def pass_on(hop, q):
        chain(hop, q).wait_recv()
        if hop < 4:
            chain(hop + 1, q).start()
            side(hop, q).start()
        if hop == 3:
            side(4, q).start()

    mine = window(x_hi, y, core)
    other_hi = window(1 - x_hi, y, core)

    own_before = window(x_hi, y + 3, core)
    own_after = window(x_hi, y + 1, core)
    other_before = window(1 - x_hi, y + 3, core)
    other_after = window(1 - x_hi, y + 1, core)
    own_far = window(x_hi, y + 2, core)
    other_far = window(1 - x_hi, y + 2, core)
    table = [
        (mine, diagonal), (mine, y_up), (mine, y_down), (other_hi, y_up), (other_hi, y_down),
        (own_before, y_up), (other_after, y_down),
        (mine, sibling), (other_hi, sibling), (own_before, sibling), (own_after, sibling),
        (other_before, sibling), (other_after, sibling), (own_far, sibling), (other_far, sibling),
        (own_before, y_up), (own_after, y_down), (own_far, across),
    ]

    def spread(q, no):
        which, device = table[no]
        src = dst = held[q].at[which]
        half = SIZES[q] // 2
        if no == 0:
            src = theirs[q]
        elif no == 15:
            src = dst = held[q].at[which, :, pl.ds(0, half)]
        elif no == 16:
            src = dst = held[q].at[which, :, pl.ds(half, half)]
        return remote(("spread", q, no), src, dst, pass_send.at[q, no], pass_recv.at[q, no], device)

    def ask():
        return remote(("ask",), offsets_ref, beside_offsets, asked_send.at[0], asked_recv.at[0], beside)

    def choose(q):
        for hop in range(5):
            side(hop, q).wait_recv()
        if q == 0:
            ask().wait_recv()
        for slot in range(K):
            offset = beside_offsets[0, slot]
            odd = lax.rem(offset, 2)
            place = offset // 2 + 5 - odd * (4 + x_lo)
            rows = near[q][place]
            theirs[q][slot] = jnp.where(chan + 1 - 2 * x_lo + offset < NB, rows, jnp.zeros_like(rows))
        spread(q, 0).start()
        for slot in range(K):
            offset = offsets_ref[0, slot]
            odd = lax.rem(offset, 2)
            place = offset // 2 + odd * (5 + x_lo)
            rows = near[q][place]
            held[q][mine, slot] = jnp.where(chan + offset < NB, rows, jnp.zeros_like(rows))
        for no in (1, 2, 7):
            spread(q, no).start()

    def other_in(q):
        spread(q, 0).wait_recv()
        for no in (3, 4, 8):
            spread(q, no).start()

    def own_before_in(q):
        spread(q, 1).wait_recv()
        spread(q, 15 if q in TURNED else 5).start()
        spread(q, 9).start()

    def own_after_in(q):
        spread(q, 2).wait_recv()
        if q in TURNED:
            spread(q, 16).start()
        spread(q, 10).start()

    def other_after_in(q):
        spread(q, 4).wait_recv()
        if q not in TURNED:
            spread(q, 6).start()
        spread(q, 12).start()

    def other_before_in(q):
        spread(q, 3).wait_recv()
        spread(q, 11).start()

    def own_far_in(q):
        if q in TURNED:
            spread(q, 15).wait_recv()
            spread(q, 16).wait_recv()
            spread(q, 17).start()
        else:
            spread(q, 5).wait_recv()
        spread(q, 13).start()

    def other_far_in(q):
        spread(q, 17 if q in TURNED else 6).wait_recv()
        spread(q, 14).start()

    def group_of(q):
        no = [first <= q < end for first, end in GROUPS].index(True)
        return no, FIRST[q] - FIRST[GROUPS[no][0]]

    def late_copy(q):
        rows = pl.ds(group_of(q)[1], SIZES[q])
        return pltpu.make_async_copy(terms[-1].at[:, :, rows], late_ref.at[:, :, rows], late_sem.at[NQ - 1 - q])

    def pair_terms(q):
        which, base = group_of(q)

        for no in range(7, 15):
            spread(q, no).wait_recv()

        def group(g, carry):
            at = pl.ds(pl.multiple_of(g * 16, 16), 16)
            right = jnp.concatenate([held[q][:, slot, at, :].reshape(256, BLK) for slot in range(K)], axis=1)
            to = pl.ds(pl.multiple_of(base + g * 16, 16), 16)
            no = FIRST[q] // 16 + g
            tile = left[
                pl.ds(pl.multiple_of(no // 4 * 128, 128), 128), pl.ds(pl.multiple_of(lax.rem(no, 4) * 256, 256), 256)
            ]
            both = jnp.dot(tile, right, preferred_element_type=F32)
            for slot in range(K):
                terms[which][slot, :, to, :] = both[:, BLK * slot : BLK * (slot + 1)].astype(BF16).reshape(8, 16, BLK)
            return carry

        lax.fori_loop(0, SIZES[q] // 16, group, 0, unroll=4)
        if which == len(GROUPS) - 1:
            late_copy(q).start()

    def sums_copy(m):
        at = pl.ds(m * 4, 4)
        return pltpu.make_async_copy(done.at[at], sums_ref.at[at], out_sem.at[m])

    def lag_sums(which, half):
        first = FIRST[GROUPS[which][0]]

        def lags(m, carry):
            at = pl.ds(m * 4, 4)
            part = jnp.concatenate([terms[which][m // 2, lax.rem(m, 2) * 4 + n].T for n in range(4)], axis=0)
            part = jnp.dot(part, lag_ref[first : first + GROUP_ROWS[which], :], preferred_element_type=F32)
            part = part.reshape(4, BLK, LAGS)
            if which > 0:
                part = total[at] + part
            if which < len(GROUPS) - 2:
                total[at] = part
            else:
                done[at] = part.astype(BF16)
                sums_copy(m).start()
            return carry

        lax.fori_loop(K * half, K * half + K, lags, 0)

    def build_left(v):
        if v == 0:
            for shift in range(1, 16):
                owner_rows(shift).wait_recv()
        lane = lax.broadcasted_iota(jnp.int32, (16, 128), 1)
        row = lax.broadcasted_iota(jnp.int32, (16, 128), 0)
        same_bin = (lane % 16) // 2 == row // 2
        even_row = row % 2 == 0
        slab = lane // 16
        even_lane = lane % 2 == 0

        def step(s, carry):
            for half in range(2):
                got = jnp.zeros((16, 128), F32)
                for w in range(8):
                    part = rows_in[half * 8 + w, :, 128 * v : 128 * v + 128].astype(F32)
                    got = jnp.where(slab == w, pltpu.roll(part, lax.rem(16 * (w + 8 - s), 128), 1), got)
                swapped = jnp.where(even_lane, pltpu.roll(got, 127, 1), -pltpu.roll(got, 1, 1))
                for h in range(2):
                    for i in range(8):
                        r = slice(h * 8 + i, h * 8 + i + 1)
                        value = jnp.where(even_row, got[r], swapped[r])
                        no = h * 32 + v * 8 + s
                        left[
                            pl.ds(pl.multiple_of(no // 4 * 128 + 16 * i, 16), 16),
                            pl.ds(pl.multiple_of(lax.rem(no, 4) * 256 + 128 * half, 128), 128),
                        ] = jnp.where(same_bin, value, 0.0).astype(BF16)
            return carry

        lax.fori_loop(0, 8, step, 0, unroll=2)

    def own_start():
        ask().start()
        for shift in range(1, 16):
            owner_rows(shift).start()

    steps = dict(
        s=begin, w=pass_on, o=own_start, a=choose, b=other_in, c=own_before_in, C=own_after_in, k=other_after_in,
        K=other_before_in, d=own_far_in, h=other_far_in, l=build_left, e=pair_terms, f=lag_sums,
    )
    for item in schedule:
        steps[item[0]](*[int(digit) for digit in item[1:]])
    for m in range(K * 2):
        sums_copy(m).wait()
    for q in range(*GROUPS[-1]):
        late_copy(q).wait()
    for key, copy in started.items():
        if key not in waited:
            copy.wait_recv()
        copy.wait_send()

def correlations_of(traces, starts, mask, pair_offsets, basis, lag_basis, schedule=SCHEDULE, name="correlate", collective_id=0):
    dma = pltpu.SemaphoreType.DMA
    return pl.pallas_call(
        functools.partial(correlate_kernel, schedule),
        name=name,
        out_shape=(
            jax.ShapeDtypeStruct((K * 8, BLK, LAGS), BF16),
            jax.ShapeDtypeStruct((K, 8, LATE, BLK), BF16),
        ),
        in_specs=[pl.BlockSpec(memory_space=pl.ANY)] * 6,
        out_specs=(pl.BlockSpec(memory_space=pl.ANY), pl.BlockSpec(memory_space=pl.ANY)),
        scratch_shapes=[pltpu.VMEM((10, size, BLK), BF16) for size in SIZES]
        + [pltpu.VMEM((16, K, size, BLK), BF16) for size in SIZES]
        + [pltpu.VMEM((K, size, BLK), BF16) for size in SIZES]
        + [pltpu.VMEM((K, 8, rows, BLK), BF16) for rows in GROUP_ROWS]
        + [
            pltpu.VMEM((16, 16, F), BF16),
            pltpu.VMEM((16, 16, F), BF16),
            pltpu.VMEM((L, ROWS), BF16),
            pltpu.VMEM((K * 8, BLK, LAGS), F32),
            pltpu.VMEM((K * 8, BLK, LAGS), BF16),
            dma((K * 2,)),
            dma((GROUPS[-1][1] - GROUPS[-1][0],)),
            pltpu.SMEM((1,), jnp.int32),
            pltpu.VMEM((BLK, SEG), BF16),
            pltpu.VMEM((1, BLK), jnp.int32),
            pltpu.SMEM((1, K), jnp.int32),
            pltpu.SMEM((1, K), jnp.int32),
            pltpu.VMEM((ROWS, LAGS), BF16),
            dma((9,)), dma((1,)), dma((1,)),
            dma((NQ, 4)), dma((NQ, 4)), dma((NQ, 5)), dma((NQ, 5)),
            dma((15,)), dma((15,)), dma((NQ, 18)), dma((NQ, 18)),
        ],
        compiler_params=pltpu.CompilerParams(
            collective_id=collective_id, has_side_effects=True, vmem_limit_bytes=VMEM_MIB * 2**20
        ),
    )(starts, traces, mask.reshape(1, BLK), pair_offsets, basis, lag_basis)


def finish_kernel(sums_hbm, late_hbm, lag_hbm, out_hbm, sums, late, lag, done, lag_sem, late_sem, sums_sem, out_sem):
    chunks = [pl.ds(m * 4, 4) for m in range(K * 2)]
    lag_in = pltpu.make_async_copy(lag_hbm.at[pl.ds(ROWS - LATE, LATE)], lag, lag_sem.at[0])
    late_in = [pltpu.make_async_copy(late_hbm.at[at], late.at[at], late_sem.at[m]) for m, at in enumerate(chunks)]
    sums_in = [pltpu.make_async_copy(sums_hbm.at[at], sums.at[at], sums_sem.at[m]) for m, at in enumerate(chunks)]
    outs = [pltpu.make_async_copy(done.at[at], out_hbm.at[at], out_sem.at[m]) for m, at in enumerate(chunks)]
    lag_in.start()
    for m in range(2):
        late_in[m].start()
        sums_in[m].start()
    lag_in.wait()
    lag_scale = 1.0 / (W * math.sqrt(F))
    for m, at in enumerate(chunks):
        late_in[m].wait()
        sums_in[m].wait()
        if m + 2 < K * 2:
            late_in[m + 2].start()
            sums_in[m + 2].start()
        part = jnp.concatenate([late[4 * m + n].T for n in range(4)], axis=0)
        part = jnp.dot(part, lag[...], preferred_element_type=F32).reshape(4, BLK, LAGS)
        done[at] = ((sums[at].astype(F32) + part) * lag_scale).astype(BF16)
        outs[m].start()
    for copy in outs:
        copy.wait()


def on_device(traces, starts, mask, pair_offsets):
    lag_basis = jnp.asarray(lag_table())
    sums, late = correlations_of(traces, starts, mask, pair_offsets, jnp.asarray(dft_table()), lag_basis)
    dma = pltpu.SemaphoreType.DMA
    out = pl.pallas_call(
        finish_kernel,
        name="finish",
        out_shape=jax.ShapeDtypeStruct((K * 8, BLK, LAGS), BF16),
        in_specs=[pl.BlockSpec(memory_space=pl.ANY)] * 3,
        out_specs=pl.BlockSpec(memory_space=pl.ANY),
        scratch_shapes=[
            pltpu.VMEM((K * 8, BLK, LAGS), BF16),
            pltpu.VMEM((K * 8, LATE, BLK), BF16),
            pltpu.VMEM((LATE, LAGS), BF16),
            pltpu.VMEM((K * 8, BLK, LAGS), BF16),
            dma((1,)), dma((K * 2,)), dma((K * 2,)), dma((K * 2,)),
        ],
        compiler_params=pltpu.CompilerParams(vmem_limit_bytes=VMEM_MIB * 2**20),
    )(sums, late.reshape(K * 8, LATE, BLK), lag_basis)
    return out.reshape(1, K, 8, BLK, LAGS)


def solution(mesh):
    in_specs = (P("chan", "freq"), P("freq"), P("chan"), P("chan", None))
    out_specs = P("chan", None, "freq", None, None)
    return jax.shard_map(
        on_device, mesh=mesh, in_specs=in_specs, out_specs=out_specs, check_vma=False
    )
```

```python
import functools
import math

import jax
import jax.numpy as jnp
import ml_dtypes
import numpy as np
from jax import lax
from jax.experimental import pallas as pl
from jax.experimental.pallas import tpu as pltpu
from jax.sharding import PartitionSpec as P

BLK = 128
NB = 16
W = 16
L = 2048
SEG = 2304
F = 512
KLO = 128
LAGS = 1024
K = 3
ROWS = 2 * F
SIZES = (128, 128, 256, 64, 128, 192, 128)
NQ = len(SIZES)
FIRST = tuple(sum(SIZES[:q]) for q in range(NQ))
TURNED = (0, 1, 2, 3, 4)
VMEM_MIB = 60
MESH = pl.DeviceIdType.MESH
BF16 = jnp.bfloat16
F32 = jnp.float32


def dft_table():
    samples = np.arange(L, dtype=np.int64)
    bin_ids = KLO + np.arange(F, dtype=np.int64)
    angles = 2.0 * np.pi / L * (samples[:, None] * bin_ids[None, :] % L)
    taper = 0.5 - 0.5 * np.cos(2.0 * np.pi / L * samples)
    both = np.stack([taper[:, None] * np.cos(angles), -taper[:, None] * np.sin(angles)], axis=2)
    return both.reshape(L, ROWS).astype(np.float32).astype(ml_dtypes.bfloat16)


def lag_table():
    bin_ids = KLO + np.arange(F, dtype=np.int64)
    delays = np.arange(LAGS, dtype=np.int64) - LAGS // 2
    angles = 2.0 * np.pi / L * (bin_ids[:, None] * delays[None, :] % L)
    both = np.stack([np.cos(angles), -np.sin(angles)], axis=1)
    return both.reshape(ROWS, LAGS).astype(np.float32).astype(ml_dtypes.bfloat16)


class Tracked:
    def __init__(self, key, copy, started, waited):
        self.key, self.copy, self.started, self.waited = key, copy, started, waited

    def start(self):
        self.copy.start()
        self.started[self.key] = self.copy

    def wait_recv(self):
        self.copy.wait_recv()
        self.waited.add(self.key)


GROUPS = ((0, 3), (3, 5), (5, 7))
GROUP_ROWS = tuple(sum(SIZES[first:end]) for first, end in GROUPS)
LATE = GROUP_ROWS[-1]

SCHEDULE = (
    "s0", "o", "w10", "s1", "w20", "l0", "w11", "s2", "l1", "w30", "l2", "w21", "l3", "w12", "s3", "w40", "a0",
    "w31", "w22", "w13", "s4", "w41", "b0", "c0", "C0", "a1", "w32", "w23", "w14", "s5", "k0", "K0", "w42", "b1",
    "d0", "w33", "a2", "w24", "c1", "C1", "w15", "s6", "w43", "k1", "K1", "h0", "a3", "w34", "e0", "w25", "w16",
    "c2", "C2", "b2", "d1", "w44", "b3", "c3", "C3", "a4", "w35", "w26", "d2", "h1", "w45", "e1", "b4", "a5",
    "w36", "K2", "k2", "K3", "k3", "d3", "c4", "C4", "w46", "h2", "K4", "k4", "a6", "e2", "b5", "c5", "h3", "C5",
    "f00", "d4", "e3", "b6", "f01", "c6", "C6", "f02", "K5", "k5", "h4", "e4", "k6", "d5", "f10", "f11", "K6",
    "f12", "h5", "d6", "h6", "e5", "e6",
)


def correlate_kernel(
    schedule, starts_hbm, traces_hbm, mask_hbm, offsets_hbm, basis_hbm, lag_hbm, sums_ref, late_ref,
    *scratch,
):
    near = scratch[:NQ]
    held = scratch[NQ : 2 * NQ]
    theirs = scratch[2 * NQ : 3 * NQ]
    terms = scratch[3 * NQ : 3 * NQ + len(GROUPS)]
    (
        by_owner, rows_in, left, total, done, out_sem, late_sem,
        starts_ref, traces_ref, mask_ref, offsets_ref, beside_offsets, lag_ref, load_sem, asked_send, asked_recv,
        chain_send, chain_recv, side_send, side_recv, own_send, own_recv, pass_send, pass_recv,
    ) = scratch[3 * NQ + len(GROUPS) :]
    basis_ref = left
    parts = [slice(n * 512, n * 512 + 512) for n in range(4)]
    operands = [
        (starts_hbm, starts_ref), (traces_hbm, traces_ref), *[(basis_hbm.at[p], basis_ref.at[p]) for p in parts],
        (mask_hbm, mask_ref), (offsets_hbm, offsets_ref), (lag_hbm, lag_ref),
    ]
    loads = [pltpu.make_async_copy(src, dst, load_sem.at[no]) for no, (src, dst) in enumerate(operands)]
    for load in loads:
        load.start()
    chan = lax.axis_index("chan")
    freq = lax.axis_index("freq")
    x_lo = lax.rem(chan, 2)
    core = lax.rem(freq, 2)
    y = lax.rem(freq // 2, 4)
    x_hi = freq // 8

    def window(hi, at_y, at_core):
        return hi * 8 + lax.rem(at_y, 4) * 2 + at_core

    below = (lax.rem(chan + 14, 16), freq)
    above = (lax.rem(chan + 2, 16), freq)
    beside = (chan + 1 - 2 * x_lo, freq)
    sibling = (chan, window(x_hi, y, 1 - core))
    across = (chan, window(1 - x_hi, y, core))
    below_beside = (lax.rem(chan + 14, 16) + 1 - 2 * x_lo, freq)
    above_beside = (lax.rem(chan + 2, 16) + 1 - 2 * x_lo, freq)
    diagonal = (chan + 1 - 2 * x_lo, window(1 - x_hi, y, core))
    y_up = (chan, window(x_hi, y + 1, core))
    y_down = (chan, window(x_hi, y + 3, core))
    peers = [(chan, lax.rem(freq + shift, 16)) for shift in range(1, 16)]

    started, waited = {}, set()
    barrier = pltpu.get_barrier_semaphore()
    everyone = peers + [below, above, beside, diagonal, below_beside, above_beside]
    for other in everyone:
        pl.semaphore_signal(barrier, inc=1, device_id=other, device_id_type=MESH)
    loads[0].wait()
    loads[1].wait()
    shifted = pltpu.roll(traces_ref[...].astype(F32), lax.rem(SEG - starts_ref[0], SEG), 1)
    segment = shifted[:, :L].astype(BF16)
    spectra = jnp.zeros((BLK, ROWS), F32)
    for n, p in enumerate(parts):
        loads[2 + n].wait()
        spectra = spectra + jnp.dot(segment[:, p], basis_ref[p, :], preferred_element_type=F32)
    for load in loads[6:]:
        load.wait()
    power_mean = jnp.sum(spectra * spectra, axis=1, keepdims=True) / F
    working = jnp.broadcast_to(mask_ref[...].astype(F32), (BLK, BLK)).T[:, :1]
    whitened = spectra * (lax.rsqrt(power_mean + 1e-06) * working)
    def turn_piece(q):
        near[q][0] = whitened[:, FIRST[q] : FIRST[q] + SIZES[q]].T.astype(BF16)

    for q in range(2):
        turn_piece(q)
    pl.semaphore_wait(barrier, len(everyone))

    def remote(key, src, dst, send, recv, device):
        copy = pltpu.make_async_remote_copy(
            src_ref=src, dst_ref=dst, send_sem=send, recv_sem=recv, device_id=device, device_id_type=MESH
        )
        return Tracked(key, copy, started, waited)

    def chain(hop, q):
        return remote(("chain", hop, q), near[q].at[hop - 1], near[q].at[hop], chain_send.at[q, hop - 1], chain_recv.at[q, hop - 1], below)

    def side(hop, q):
        src, device = (hop, beside) if hop < 4 else (3, below_beside)
        return remote(("side", hop, q), near[q].at[src], near[q].at[5 + hop], side_send.at[q, hop], side_recv.at[q, hop], device)

    def owner_rows(shift):
        there = lax.rem(freq + shift, 16)
        return remote(("own", shift), by_owner.at[there], rows_in.at[freq], own_send.at[shift - 1], own_recv.at[shift - 1], (chan, there))

    def begin(q):
        if q >= 2:
            turn_piece(q)
        chain(1, q).start()
        side(0, q).start()

    def pass_on(hop, q):
        chain(hop, q).wait_recv()
        if hop < 4:
            chain(hop + 1, q).start()
            side(hop, q).start()
        if hop == 3:
            side(4, q).start()

    mine = window(x_hi, y, core)
    other_hi = window(1 - x_hi, y, core)

    own_before = window(x_hi, y + 3, core)
    own_after = window(x_hi, y + 1, core)
    other_before = window(1 - x_hi, y + 3, core)
    other_after = window(1 - x_hi, y + 1, core)
    own_far = window(x_hi, y + 2, core)
    other_far = window(1 - x_hi, y + 2, core)
    table = [
        (mine, diagonal), (mine, y_up), (mine, y_down), (other_hi, y_up), (other_hi, y_down),
        (own_before, y_up), (other_after, y_down),
        (mine, sibling), (other_hi, sibling), (own_before, sibling), (own_after, sibling),
        (other_before, sibling), (other_after, sibling), (own_far, sibling), (other_far, sibling),
        (own_before, y_up), (own_after, y_down), (own_far, across),
    ]

    def spread(q, no):
        which, device = table[no]
        src = dst = held[q].at[which]
        half = SIZES[q] // 2
        if no == 0:
            src = theirs[q]
        elif no == 15:
            src = dst = held[q].at[which, :, pl.ds(0, half)]
        elif no == 16:
            src = dst = held[q].at[which, :, pl.ds(half, half)]
        return remote(("spread", q, no), src, dst, pass_send.at[q, no], pass_recv.at[q, no], device)

    def ask():
        return remote(("ask",), offsets_ref, beside_offsets, asked_send.at[0], asked_recv.at[0], beside)

    def choose(q):
        for hop in range(5):
            side(hop, q).wait_recv()
        if q == 0:
            ask().wait_recv()
        for slot in range(K):
            offset = beside_offsets[0, slot]
            odd = lax.rem(offset, 2)
            place = offset // 2 + 5 - odd * (4 + x_lo)
            rows = near[q][place]
            theirs[q][slot] = jnp.where(chan + 1 - 2 * x_lo + offset < NB, rows, jnp.zeros_like(rows))
        spread(q, 0).start()
        for slot in range(K):
            offset = offsets_ref[0, slot]
            odd = lax.rem(offset, 2)
            place = offset // 2 + odd * (5 + x_lo)
            rows = near[q][place]
            held[q][mine, slot] = jnp.where(chan + offset < NB, rows, jnp.zeros_like(rows))
        for no in (1, 2, 7):
            spread(q, no).start()

    def other_in(q):
        spread(q, 0).wait_recv()
        for no in (3, 4, 8):
            spread(q, no).start()

    def own_before_in(q):
        spread(q, 1).wait_recv()
        spread(q, 15 if q in TURNED else 5).start()
        spread(q, 9).start()

    def own_after_in(q):
        spread(q, 2).wait_recv()
        if q in TURNED:
            spread(q, 16).start()
        spread(q, 10).start()

    def other_after_in(q):
        spread(q, 4).wait_recv()
        if q not in TURNED:
            spread(q, 6).start()
        spread(q, 12).start()

    def other_before_in(q):
        spread(q, 3).wait_recv()
        spread(q, 11).start()

    def own_far_in(q):
        if q in TURNED:
            spread(q, 15).wait_recv()
            spread(q, 16).wait_recv()
            spread(q, 17).start()
        else:
            spread(q, 5).wait_recv()
        spread(q, 13).start()

    def other_far_in(q):
        spread(q, 17 if q in TURNED else 6).wait_recv()
        spread(q, 14).start()

    def group_of(q):
        no = [first <= q < end for first, end in GROUPS].index(True)
        return no, FIRST[q] - FIRST[GROUPS[no][0]]

    def late_copy(q):
        rows = pl.ds(group_of(q)[1], SIZES[q])
        return pltpu.make_async_copy(terms[-1].at[:, :, rows], late_ref.at[:, :, rows], late_sem.at[NQ - 1 - q])

    def pair_terms(q):
        which, base = group_of(q)

        for no in range(7, 15):
            spread(q, no).wait_recv()

        def group(g, carry):
            at = pl.ds(pl.multiple_of(g * 16, 16), 16)
            right = jnp.concatenate([held[q][:, slot, at, :].reshape(256, BLK) for slot in range(K)], axis=1)
            to = pl.ds(pl.multiple_of(base + g * 16, 16), 16)
            no = FIRST[q] // 16 + g
            tile = left[
                pl.ds(pl.multiple_of(no // 4 * 128, 128), 128), pl.ds(pl.multiple_of(lax.rem(no, 4) * 256, 256), 256)
            ]
            both = jnp.dot(tile, right, preferred_element_type=F32)
            for slot in range(K):
                terms[which][slot, :, to, :] = both[:, BLK * slot : BLK * (slot + 1)].astype(BF16).reshape(8, 16, BLK)
            return carry

        lax.fori_loop(0, SIZES[q] // 16, group, 0, unroll=4)
        if which == len(GROUPS) - 1:
            late_copy(q).start()

    def sums_copy(m):
        at = pl.ds(m * 4, 4)
        return pltpu.make_async_copy(done.at[at], sums_ref.at[at], out_sem.at[m])

    def lag_sums(which, part_no):
        first = FIRST[GROUPS[which][0]]

        def lags(m, carry):
            at = pl.ds(m * 4, 4)
            part = jnp.concatenate([terms[which][m // 2, lax.rem(m, 2) * 4 + n].T for n in range(4)], axis=0)
            part = jnp.dot(part, lag_ref[first : first + GROUP_ROWS[which], :], preferred_element_type=F32)
            part = part.reshape(4, BLK, LAGS)
            if which > 0:
                part = total[at] + part
            if which < len(GROUPS) - 2:
                total[at] = part
            else:
                done[at] = part.astype(BF16)
                sums_copy(m).start()
            return carry

        lax.fori_loop(2 * part_no, 2 * part_no + 2, lags, 0)

    def build_left(v):
        if v == 0:
            for shift in range(1, 16):
                owner_rows(shift).wait_recv()
        lane = lax.broadcasted_iota(jnp.int32, (16, 128), 1)
        row = lax.broadcasted_iota(jnp.int32, (16, 128), 0)
        same_bin = (lane % 16) // 2 == row // 2
        even_row = row % 2 == 0
        slab = lane // 16
        even_lane = lane % 2 == 0

        def step(s, carry):
            for half in range(2):
                got = jnp.zeros((16, 128), F32)
                for w in range(8):
                    part = rows_in[half * 8 + w, :, 128 * v : 128 * v + 128].astype(F32)
                    got = jnp.where(slab == w, pltpu.roll(part, lax.rem(16 * (w + 8 - s), 128), 1), got)
                swapped = jnp.where(even_lane, pltpu.roll(got, 127, 1), -pltpu.roll(got, 1, 1))
                for h in range(2):
                    for i in range(8):
                        r = slice(h * 8 + i, h * 8 + i + 1)
                        value = jnp.where(even_row, got[r], swapped[r])
                        no = h * 32 + v * 8 + s
                        left[
                            pl.ds(pl.multiple_of(no // 4 * 128 + 16 * i, 16), 16),
                            pl.ds(pl.multiple_of(lax.rem(no, 4) * 256 + 128 * half, 128), 128),
                        ] = jnp.where(same_bin, value, 0.0).astype(BF16)
            return carry

        lax.fori_loop(0, 8, step, 0, unroll=2)

    def own_start():
        for owner in range(16):
            rows = whitened[8 * owner : 8 * owner + 8]
            by_owner[owner] = jnp.concatenate([rows[:, :F], rows[:, F:]], axis=0).astype(BF16)
        rows_in[freq] = by_owner[freq]
        ask().start()
        for shift in range(1, 16):
            owner_rows(shift).start()

    steps = dict(
        s=begin, w=pass_on, o=own_start, a=choose, b=other_in, c=own_before_in, C=own_after_in, k=other_after_in,
        K=other_before_in, d=own_far_in, h=other_far_in, l=build_left, e=pair_terms, f=lag_sums,
    )
    for item in schedule:
        steps[item[0]](*[int(digit) for digit in item[1:]])
    for m in range(K * 2):
        sums_copy(m).wait()
    for q in range(*GROUPS[-1]):
        late_copy(q).wait()
    for key, copy in started.items():
        if key not in waited:
            copy.wait_recv()
        copy.wait_send()

def correlations_of(traces, starts, mask, pair_offsets, basis, lag_basis, schedule=SCHEDULE, name="correlate", collective_id=0):
    dma = pltpu.SemaphoreType.DMA
    return pl.pallas_call(
        functools.partial(correlate_kernel, schedule),
        name=name,
        out_shape=(
            jax.ShapeDtypeStruct((K * 8, BLK, LAGS), BF16),
            jax.ShapeDtypeStruct((K, 8, LATE, BLK), BF16),
        ),
        in_specs=[pl.BlockSpec(memory_space=pl.ANY)] * 6,
        out_specs=(pl.BlockSpec(memory_space=pl.ANY), pl.BlockSpec(memory_space=pl.ANY)),
        scratch_shapes=[pltpu.VMEM((10, size, BLK), BF16) for size in SIZES]
        + [pltpu.VMEM((16, K, size, BLK), BF16) for size in SIZES]
        + [pltpu.VMEM((K, size, BLK), BF16) for size in SIZES]
        + [pltpu.VMEM((K, 8, rows, BLK), BF16) for rows in GROUP_ROWS]
        + [
            pltpu.VMEM((16, 16, F), BF16),
            pltpu.VMEM((16, 16, F), BF16),
            pltpu.VMEM((L, ROWS), BF16),
            pltpu.VMEM((K * 8, BLK, LAGS), F32),
            pltpu.VMEM((K * 8, BLK, LAGS), BF16),
            dma((K * 2,)),
            dma((GROUPS[-1][1] - GROUPS[-1][0],)),
            pltpu.SMEM((1,), jnp.int32),
            pltpu.VMEM((BLK, SEG), BF16),
            pltpu.VMEM((1, BLK), jnp.int32),
            pltpu.SMEM((1, K), jnp.int32),
            pltpu.SMEM((1, K), jnp.int32),
            pltpu.VMEM((ROWS, LAGS), BF16),
            dma((9,)), dma((1,)), dma((1,)),
            dma((NQ, 4)), dma((NQ, 4)), dma((NQ, 5)), dma((NQ, 5)),
            dma((15,)), dma((15,)), dma((NQ, 18)), dma((NQ, 18)),
        ],
        compiler_params=pltpu.CompilerParams(
            collective_id=collective_id, has_side_effects=True, vmem_limit_bytes=VMEM_MIB * 2**20
        ),
    )(starts, traces, mask.reshape(1, BLK), pair_offsets, basis, lag_basis)


def finish_kernel(sums_hbm, late_hbm, lag_hbm, out_hbm, sums, late, lag, done, lag_sem, late_sem, sums_sem, out_sem):
    chunks = [pl.ds(m * 4, 4) for m in range(K * 2)]
    lag_in = pltpu.make_async_copy(lag_hbm.at[pl.ds(ROWS - LATE, LATE)], lag, lag_sem.at[0])
    late_in = [pltpu.make_async_copy(late_hbm.at[at], late.at[at], late_sem.at[m]) for m, at in enumerate(chunks)]
    sums_in = [pltpu.make_async_copy(sums_hbm.at[at], sums.at[at], sums_sem.at[m]) for m, at in enumerate(chunks)]
    outs = [pltpu.make_async_copy(done.at[at], out_hbm.at[at], out_sem.at[m]) for m, at in enumerate(chunks)]
    lag_in.start()
    for m in range(2):
        late_in[m].start()
        sums_in[m].start()
    lag_in.wait()
    lag_scale = 1.0 / (W * math.sqrt(F))
    for m, at in enumerate(chunks):
        late_in[m].wait()
        sums_in[m].wait()
        if m + 2 < K * 2:
            late_in[m + 2].start()
            sums_in[m + 2].start()
        part = jnp.concatenate([late[4 * m + n].T for n in range(4)], axis=0)
        part = jnp.dot(part, lag[...], preferred_element_type=F32).reshape(4, BLK, LAGS)
        done[at] = ((sums[at].astype(F32) + part) * lag_scale).astype(BF16)
        outs[m].start()
    for copy in outs:
        copy.wait()


def on_device(traces, starts, mask, pair_offsets):
    lag_basis = jnp.asarray(lag_table())
    sums, late = correlations_of(traces, starts, mask, pair_offsets, jnp.asarray(dft_table()), lag_basis)
    dma = pltpu.SemaphoreType.DMA
    out = pl.pallas_call(
        finish_kernel,
        name="finish",
        out_shape=jax.ShapeDtypeStruct((K * 8, BLK, LAGS), BF16),
        in_specs=[pl.BlockSpec(memory_space=pl.ANY)] * 3,
        out_specs=pl.BlockSpec(memory_space=pl.ANY),
        scratch_shapes=[
            pltpu.VMEM((K * 8, BLK, LAGS), BF16),
            pltpu.VMEM((K * 8, LATE, BLK), BF16),
            pltpu.VMEM((LATE, LAGS), BF16),
            pltpu.VMEM((K * 8, BLK, LAGS), BF16),
            dma((1,)), dma((K * 2,)), dma((K * 2,)), dma((K * 2,)),
        ],
        compiler_params=pltpu.CompilerParams(vmem_limit_bytes=VMEM_MIB * 2**20),
    )(sums, late.reshape(K * 8, LATE, BLK), lag_basis)
    return out.reshape(1, K, 8, BLK, LAGS)


def solution(mesh):
    in_specs = (P("chan", "freq"), P("freq"), P("chan"), P("chan", None))
    out_specs = P("chan", None, "freq", None, None)
    return jax.shard_map(
        on_device, mesh=mesh, in_specs=in_specs, out_specs=out_specs, check_vma=False
    )
```

```python
import functools
import math

import jax
import jax.numpy as jnp
import ml_dtypes
import numpy as np
from jax import lax
from jax.experimental import pallas as pl
from jax.experimental.pallas import tpu as pltpu
from jax.sharding import PartitionSpec as P

BLK = 128
NB = 16
W = 16
L = 2048
SEG = 2304
F = 512
KLO = 128
LAGS = 1024
K = 3
ROWS = 2 * F
SIZES = (128, 192, 192, 64, 192, 128, 128)
NQ = len(SIZES)
FIRST = tuple(sum(SIZES[:q]) for q in range(NQ))
TURNED = (0, 1, 2, 3, 4)
VMEM_MIB = 60
MESH = pl.DeviceIdType.MESH
BF16 = jnp.bfloat16
F32 = jnp.float32


def dft_table():
    samples = np.arange(L, dtype=np.int64)
    bin_ids = KLO + np.arange(F, dtype=np.int64)
    angles = 2.0 * np.pi / L * (samples[:, None] * bin_ids[None, :] % L)
    taper = 0.5 - 0.5 * np.cos(2.0 * np.pi / L * samples)
    both = np.stack([taper[:, None] * np.cos(angles), -taper[:, None] * np.sin(angles)], axis=2)
    return both.reshape(L, ROWS).astype(np.float32).astype(ml_dtypes.bfloat16)


def lag_table():
    bin_ids = KLO + np.arange(F, dtype=np.int64)
    delays = np.arange(LAGS, dtype=np.int64) - LAGS // 2
    angles = 2.0 * np.pi / L * (bin_ids[:, None] * delays[None, :] % L)
    both = np.stack([np.cos(angles), -np.sin(angles)], axis=1)
    return both.reshape(ROWS, LAGS).astype(np.float32).astype(ml_dtypes.bfloat16)


class Tracked:
    def __init__(self, key, copy, started, waited):
        self.key, self.copy, self.started, self.waited = key, copy, started, waited

    def start(self):
        self.copy.start()
        self.started[self.key] = self.copy

    def wait_recv(self):
        self.copy.wait_recv()
        self.waited.add(self.key)


GROUPS = ((0, 3), (3, 5), (5, 7))
GROUP_ROWS = tuple(sum(SIZES[first:end]) for first, end in GROUPS)
LATE = GROUP_ROWS[-1]

SCHEDULE = (
    "s0", "o", "w10", "s1", "w20", "l0", "w11", "s2", "l1", "w30", "l2", "l3", "w21", "w12", "s3", "w40", "a0",
    "w31", "w22", "w13", "s4", "b0", "c0", "C0", "w41", "a1", "w32", "w23", "w14", "s5", "k0", "K0", "d0", "w42",
    "w33", "a2", "b1", "w24", "c1", "C1", "w15", "s6", "w43", "h0", "a3", "w34", "e0", "c2", "C2", "w25", "w16",
    "b2", "b3", "w44", "k1", "K1", "a4", "w35", "d1", "w26", "c3", "C3", "d2", "w45", "a5", "w36", "b4", "k2",
    "K2", "k3", "K3", "w46", "h1", "c4", "C4", "d3", "e1", "c5", "C5", "h2", "a6", "b5", "e2", "k4", "K4", "h3",
    "d4", "f00", "f01", "d5", "b6", "C6", "e3", "f02", "c6", "k5", "h4", "K5", "e4", "k6", "K6", "f10", "h5",
    "f11", "d6", "f12", "e5", "h6", "e6",
)


def correlate_kernel(
    schedule, starts_hbm, traces_hbm, mask_hbm, offsets_hbm, basis_hbm, lag_hbm, sums_ref, late_ref,
    *scratch,
):
    near = scratch[:NQ]
    held = scratch[NQ : 2 * NQ]
    theirs = scratch[2 * NQ : 3 * NQ]
    terms = scratch[3 * NQ : 3 * NQ + len(GROUPS)]
    (
        by_owner, rows_in, left, total, done, out_sem, late_sem,
        starts_ref, traces_ref, mask_ref, offsets_ref, beside_offsets, lag_ref, load_sem, asked_send, asked_recv,
        chain_send, chain_recv, side_send, side_recv, own_send, own_recv, pass_send, pass_recv,
    ) = scratch[3 * NQ + len(GROUPS) :]
    basis_ref = left
    parts = [slice(n * 512, n * 512 + 512) for n in range(4)]
    operands = [
        (starts_hbm, starts_ref), (traces_hbm, traces_ref), *[(basis_hbm.at[p], basis_ref.at[p]) for p in parts],
        (mask_hbm, mask_ref), (offsets_hbm, offsets_ref), (lag_hbm, lag_ref),
    ]
    loads = [pltpu.make_async_copy(src, dst, load_sem.at[no]) for no, (src, dst) in enumerate(operands)]
    for load in loads:
        load.start()
    chan = lax.axis_index("chan")
    freq = lax.axis_index("freq")
    x_lo = lax.rem(chan, 2)
    core = lax.rem(freq, 2)
    y = lax.rem(freq // 2, 4)
    x_hi = freq // 8

    def window(hi, at_y, at_core):
        return hi * 8 + lax.rem(at_y, 4) * 2 + at_core

    below = (lax.rem(chan + 14, 16), freq)
    above = (lax.rem(chan + 2, 16), freq)
    beside = (chan + 1 - 2 * x_lo, freq)
    sibling = (chan, window(x_hi, y, 1 - core))
    across = (chan, window(1 - x_hi, y, core))
    below_beside = (lax.rem(chan + 14, 16) + 1 - 2 * x_lo, freq)
    above_beside = (lax.rem(chan + 2, 16) + 1 - 2 * x_lo, freq)
    diagonal = (chan + 1 - 2 * x_lo, window(1 - x_hi, y, core))
    y_up = (chan, window(x_hi, y + 1, core))
    y_down = (chan, window(x_hi, y + 3, core))
    peers = [(chan, lax.rem(freq + shift, 16)) for shift in range(1, 16)]

    started, waited = {}, set()
    barrier = pltpu.get_barrier_semaphore()
    everyone = peers + [below, above, beside, diagonal, below_beside, above_beside]
    for other in everyone:
        pl.semaphore_signal(barrier, inc=1, device_id=other, device_id_type=MESH)
    loads[0].wait()
    loads[1].wait()
    shifted = pltpu.roll(traces_ref[...].astype(F32), lax.rem(SEG - starts_ref[0], SEG), 1)
    segment = shifted[:, :L].astype(BF16)
    spectra = jnp.zeros((BLK, ROWS), F32)
    for n, p in enumerate(parts):
        loads[2 + n].wait()
        spectra = spectra + jnp.dot(segment[:, p], basis_ref[p, :], preferred_element_type=F32)
    for load in loads[6:]:
        load.wait()
    power_mean = jnp.sum(spectra * spectra, axis=1, keepdims=True) / F
    working = jnp.broadcast_to(mask_ref[...].astype(F32), (BLK, BLK)).T[:, :1]
    whitened = spectra * (lax.rsqrt(power_mean + 1e-06) * working)
    def turn_piece(q):
        near[q][0] = whitened[:, FIRST[q] : FIRST[q] + SIZES[q]].T.astype(BF16)

    for q in range(2):
        turn_piece(q)
    pl.semaphore_wait(barrier, len(everyone))

    def remote(key, src, dst, send, recv, device):
        copy = pltpu.make_async_remote_copy(
            src_ref=src, dst_ref=dst, send_sem=send, recv_sem=recv, device_id=device, device_id_type=MESH
        )
        return Tracked(key, copy, started, waited)

    def chain(hop, q):
        return remote(("chain", hop, q), near[q].at[hop - 1], near[q].at[hop], chain_send.at[q, hop - 1], chain_recv.at[q, hop - 1], below)

    def side(hop, q):
        src, device = (hop, beside) if hop < 4 else (3, below_beside)
        return remote(("side", hop, q), near[q].at[src], near[q].at[5 + hop], side_send.at[q, hop], side_recv.at[q, hop], device)

    def owner_rows(shift):
        there = lax.rem(freq + shift, 16)
        return remote(("own", shift), by_owner.at[there], rows_in.at[freq], own_send.at[shift - 1], own_recv.at[shift - 1], (chan, there))

    def begin(q):
        if q >= 2:
            turn_piece(q)
        chain(1, q).start()
        side(0, q).start()

    def pass_on(hop, q):
        chain(hop, q).wait_recv()
        if hop < 4:
            chain(hop + 1, q).start()
            side(hop, q).start()
        if hop == 3:
            side(4, q).start()

    mine = window(x_hi, y, core)
    other_hi = window(1 - x_hi, y, core)

    own_before = window(x_hi, y + 3, core)
    own_after = window(x_hi, y + 1, core)
    other_before = window(1 - x_hi, y + 3, core)
    other_after = window(1 - x_hi, y + 1, core)
    own_far = window(x_hi, y + 2, core)
    other_far = window(1 - x_hi, y + 2, core)
    table = [
        (mine, diagonal), (mine, y_up), (mine, y_down), (other_hi, y_up), (other_hi, y_down),
        (own_before, y_up), (other_after, y_down),
        (mine, sibling), (other_hi, sibling), (own_before, sibling), (own_after, sibling),
        (other_before, sibling), (other_after, sibling), (own_far, sibling), (other_far, sibling),
        (own_before, y_up), (own_after, y_down), (own_far, across),
    ]

    def spread(q, no):
        which, device = table[no]
        src = dst = held[q].at[which]
        half = SIZES[q] // 2
        if no == 0:
            src = theirs[q]
        elif no == 15:
            src = dst = held[q].at[which, :, pl.ds(0, half)]
        elif no == 16:
            src = dst = held[q].at[which, :, pl.ds(half, half)]
        return remote(("spread", q, no), src, dst, pass_send.at[q, no], pass_recv.at[q, no], device)

    def ask():
        return remote(("ask",), offsets_ref, beside_offsets, asked_send.at[0], asked_recv.at[0], beside)

    def choose(q):
        for hop in range(5):
            side(hop, q).wait_recv()
        if q == 0:
            ask().wait_recv()
        for slot in range(K):
            offset = beside_offsets[0, slot]
            odd = lax.rem(offset, 2)
            place = offset // 2 + 5 - odd * (4 + x_lo)
            rows = near[q][place]
            theirs[q][slot] = jnp.where(chan + 1 - 2 * x_lo + offset < NB, rows, jnp.zeros_like(rows))
        spread(q, 0).start()
        for slot in range(K):
            offset = offsets_ref[0, slot]
            odd = lax.rem(offset, 2)
            place = offset // 2 + odd * (5 + x_lo)
            rows = near[q][place]
            held[q][mine, slot] = jnp.where(chan + offset < NB, rows, jnp.zeros_like(rows))
        for no in (1, 2, 7):
            spread(q, no).start()

    def other_in(q):
        spread(q, 0).wait_recv()
        for no in (3, 4, 8):
            spread(q, no).start()

    def own_before_in(q):
        spread(q, 1).wait_recv()
        spread(q, 15 if q in TURNED else 5).start()
        spread(q, 9).start()

    def own_after_in(q):
        spread(q, 2).wait_recv()
        if q in TURNED:
            spread(q, 16).start()
        spread(q, 10).start()

    def other_after_in(q):
        spread(q, 4).wait_recv()
        if q not in TURNED:
            spread(q, 6).start()
        spread(q, 12).start()

    def other_before_in(q):
        spread(q, 3).wait_recv()
        spread(q, 11).start()

    def own_far_in(q):
        if q in TURNED:
            spread(q, 15).wait_recv()
            spread(q, 16).wait_recv()
            spread(q, 17).start()
        else:
            spread(q, 5).wait_recv()
        spread(q, 13).start()

    def other_far_in(q):
        spread(q, 17 if q in TURNED else 6).wait_recv()
        spread(q, 14).start()

    def group_of(q):
        no = [first <= q < end for first, end in GROUPS].index(True)
        return no, FIRST[q] - FIRST[GROUPS[no][0]]

    def late_copy(q):
        rows = pl.ds(group_of(q)[1], SIZES[q])
        return pltpu.make_async_copy(terms[-1].at[:, :, rows], late_ref.at[:, :, rows], late_sem.at[NQ - 1 - q])

    def pair_terms(q):
        which, base = group_of(q)

        for no in range(7, 15):
            spread(q, no).wait_recv()

        def group(g, carry):
            at = pl.ds(pl.multiple_of(g * 16, 16), 16)
            right = jnp.concatenate([held[q][:, slot, at, :].reshape(256, BLK) for slot in range(K)], axis=1)
            to = pl.ds(pl.multiple_of(base + g * 16, 16), 16)
            no = FIRST[q] // 16 + g
            tile = left[
                pl.ds(pl.multiple_of(no // 4 * 128, 128), 128), pl.ds(pl.multiple_of(lax.rem(no, 4) * 256, 256), 256)
            ]
            both = jnp.dot(tile, right, preferred_element_type=F32)
            for slot in range(K):
                terms[which][slot, :, to, :] = both[:, BLK * slot : BLK * (slot + 1)].astype(BF16).reshape(8, 16, BLK)
            return carry

        lax.fori_loop(0, SIZES[q] // 16, group, 0, unroll=4)
        if which == len(GROUPS) - 1:
            late_copy(q).start()

    def sums_copy(m):
        at = pl.ds(m * 4, 4)
        return pltpu.make_async_copy(done.at[at], sums_ref.at[at], out_sem.at[m])

    def lag_sums(which, part_no):
        first = FIRST[GROUPS[which][0]]

        def lags(m, carry):
            at = pl.ds(m * 4, 4)
            part = jnp.concatenate([terms[which][m // 2, lax.rem(m, 2) * 4 + n].T for n in range(4)], axis=0)
            part = jnp.dot(part, lag_ref[first : first + GROUP_ROWS[which], :], preferred_element_type=F32)
            part = part.reshape(4, BLK, LAGS)
            if which > 0:
                part = total[at] + part
            if which < len(GROUPS) - 2:
                total[at] = part
            else:
                done[at] = part.astype(BF16)
                sums_copy(m).start()
            return carry

        lax.fori_loop(2 * part_no, 2 * part_no + 2, lags, 0)

    def build_left(v):
        if v == 0:
            for shift in range(1, 16):
                owner_rows(shift).wait_recv()
        lane = lax.broadcasted_iota(jnp.int32, (16, 128), 1)
        row = lax.broadcasted_iota(jnp.int32, (16, 128), 0)
        same_bin = (lane % 16) // 2 == row // 2
        even_row = row % 2 == 0
        slab = lane // 16
        even_lane = lane % 2 == 0

        def step(s, carry):
            for half in range(2):
                got = jnp.zeros((16, 128), F32)
                for w in range(8):
                    part = rows_in[half * 8 + w, :, 128 * v : 128 * v + 128].astype(F32)
                    got = jnp.where(slab == w, pltpu.roll(part, lax.rem(16 * (w + 8 - s), 128), 1), got)
                swapped = jnp.where(even_lane, pltpu.roll(got, 127, 1), -pltpu.roll(got, 1, 1))
                for h in range(2):
                    for i in range(8):
                        r = slice(h * 8 + i, h * 8 + i + 1)
                        value = jnp.where(even_row, got[r], swapped[r])
                        no = h * 32 + v * 8 + s
                        left[
                            pl.ds(pl.multiple_of(no // 4 * 128 + 16 * i, 16), 16),
                            pl.ds(pl.multiple_of(lax.rem(no, 4) * 256 + 128 * half, 128), 128),
                        ] = jnp.where(same_bin, value, 0.0).astype(BF16)
            return carry

        lax.fori_loop(0, 8, step, 0, unroll=2)

    def own_start():
        for owner in range(16):
            rows = whitened[8 * owner : 8 * owner + 8]
            by_owner[owner] = jnp.concatenate([rows[:, :F], rows[:, F:]], axis=0).astype(BF16)
        rows_in[freq] = by_owner[freq]
        ask().start()
        for shift in range(1, 16):
            owner_rows(shift).start()

    steps = dict(
        s=begin, w=pass_on, o=own_start, a=choose, b=other_in, c=own_before_in, C=own_after_in, k=other_after_in,
        K=other_before_in, d=own_far_in, h=other_far_in, l=build_left, e=pair_terms, f=lag_sums,
    )
    for item in schedule:
        steps[item[0]](*[int(digit) for digit in item[1:]])
    for m in range(K * 2):
        sums_copy(m).wait()
    for q in range(*GROUPS[-1]):
        late_copy(q).wait()
    for key, copy in started.items():
        if key not in waited:
            copy.wait_recv()
        copy.wait_send()

def correlations_of(traces, starts, mask, pair_offsets, basis, lag_basis, schedule=SCHEDULE, name="correlate", collective_id=0):
    dma = pltpu.SemaphoreType.DMA
    return pl.pallas_call(
        functools.partial(correlate_kernel, schedule),
        name=name,
        out_shape=(
            jax.ShapeDtypeStruct((K * 8, BLK, LAGS), BF16),
            jax.ShapeDtypeStruct((K, 8, LATE, BLK), BF16),
        ),
        in_specs=[pl.BlockSpec(memory_space=pl.ANY)] * 6,
        out_specs=(pl.BlockSpec(memory_space=pl.ANY), pl.BlockSpec(memory_space=pl.ANY)),
        scratch_shapes=[pltpu.VMEM((10, size, BLK), BF16) for size in SIZES]
        + [pltpu.VMEM((16, K, size, BLK), BF16) for size in SIZES]
        + [pltpu.VMEM((K, size, BLK), BF16) for size in SIZES]
        + [pltpu.VMEM((K, 8, rows, BLK), BF16) for rows in GROUP_ROWS]
        + [
            pltpu.VMEM((16, 16, F), BF16),
            pltpu.VMEM((16, 16, F), BF16),
            pltpu.VMEM((L, ROWS), BF16),
            pltpu.VMEM((K * 8, BLK, LAGS), F32),
            pltpu.VMEM((K * 8, BLK, LAGS), BF16),
            dma((K * 2,)),
            dma((GROUPS[-1][1] - GROUPS[-1][0],)),
            pltpu.SMEM((1,), jnp.int32),
            pltpu.VMEM((BLK, SEG), BF16),
            pltpu.VMEM((1, BLK), jnp.int32),
            pltpu.SMEM((1, K), jnp.int32),
            pltpu.SMEM((1, K), jnp.int32),
            pltpu.VMEM((ROWS, LAGS), BF16),
            dma((9,)), dma((1,)), dma((1,)),
            dma((NQ, 4)), dma((NQ, 4)), dma((NQ, 5)), dma((NQ, 5)),
            dma((15,)), dma((15,)), dma((NQ, 18)), dma((NQ, 18)),
        ],
        compiler_params=pltpu.CompilerParams(
            collective_id=collective_id, has_side_effects=True, vmem_limit_bytes=VMEM_MIB * 2**20
        ),
    )(starts, traces, mask.reshape(1, BLK), pair_offsets, basis, lag_basis)


def finish_kernel(sums_hbm, late_hbm, lag_hbm, out_hbm, sums, late, lag, done, lag_sem, late_sem, sums_sem, out_sem):
    chunks = [pl.ds(m * 4, 4) for m in range(K * 2)]
    lag_in = pltpu.make_async_copy(lag_hbm.at[pl.ds(ROWS - LATE, LATE)], lag, lag_sem.at[0])
    late_in = [pltpu.make_async_copy(late_hbm.at[at], late.at[at], late_sem.at[m]) for m, at in enumerate(chunks)]
    sums_in = [pltpu.make_async_copy(sums_hbm.at[at], sums.at[at], sums_sem.at[m]) for m, at in enumerate(chunks)]
    outs = [pltpu.make_async_copy(done.at[at], out_hbm.at[at], out_sem.at[m]) for m, at in enumerate(chunks)]
    lag_in.start()
    for m in range(2):
        late_in[m].start()
        sums_in[m].start()
    lag_in.wait()
    lag_scale = 1.0 / (W * math.sqrt(F))
    for m, at in enumerate(chunks):
        late_in[m].wait()
        sums_in[m].wait()
        if m + 2 < K * 2:
            late_in[m + 2].start()
            sums_in[m + 2].start()
        part = jnp.concatenate([late[4 * m + n].T for n in range(4)], axis=0)
        part = jnp.dot(part, lag[...], preferred_element_type=F32).reshape(4, BLK, LAGS)
        done[at] = ((sums[at].astype(F32) + part) * lag_scale).astype(BF16)
        outs[m].start()
    for copy in outs:
        copy.wait()


def on_device(traces, starts, mask, pair_offsets):
    lag_basis = jnp.asarray(lag_table())
    sums, late = correlations_of(traces, starts, mask, pair_offsets, jnp.asarray(dft_table()), lag_basis)
    dma = pltpu.SemaphoreType.DMA
    out = pl.pallas_call(
        finish_kernel,
        name="finish",
        out_shape=jax.ShapeDtypeStruct((K * 8, BLK, LAGS), BF16),
        in_specs=[pl.BlockSpec(memory_space=pl.ANY)] * 3,
        out_specs=pl.BlockSpec(memory_space=pl.ANY),
        scratch_shapes=[
            pltpu.VMEM((K * 8, BLK, LAGS), BF16),
            pltpu.VMEM((K * 8, LATE, BLK), BF16),
            pltpu.VMEM((LATE, LAGS), BF16),
            pltpu.VMEM((K * 8, BLK, LAGS), BF16),
            dma((1,)), dma((K * 2,)), dma((K * 2,)), dma((K * 2,)),
        ],
        compiler_params=pltpu.CompilerParams(vmem_limit_bytes=VMEM_MIB * 2**20),
    )(sums, late.reshape(K * 8, LATE, BLK), lag_basis)
    return out.reshape(1, K, 8, BLK, LAGS)


def solution(mesh):
    in_specs = (P("chan", "freq"), P("freq"), P("chan"), P("chan", None))
    out_specs = P("chan", None, "freq", None, None)
    return jax.shard_map(
        on_device, mesh=mesh, in_specs=in_specs, out_specs=out_specs, check_vma=False
    )
```
